256 devices in a mesh: ctx: 16 (over z, x_lo), exp: 16 (over x_hi, y, core).
Axes of the slice: x: 4 (x_hi: 2, x_lo: 2; x = x_hi * 2 + x_lo), y: 4, z: 8, core: 2. Of those that a mesh axis runs over, the one named last changes fastest.
Arguments:
- queries: bfloat16 [4096, 36864], P('ctx', 'exp'), may hold values from -8 to 8
- latent: bfloat16 [4096, 576], P('ctx'), may hold values from -8 to 8
- block_order: int32 [32], replicated, may hold values from 0 to 31, each once
- w_uv: bfloat16 [64, 512, 128], P('exp'), may hold values from -0.25 to 0.25
- w_o: bfloat16 [8192, 7168], P('exp', 'ctx'), may hold values from -0.0625 to 0.0625
- residual: bfloat16 [4096, 7168], P(('ctx', 'exp')), may hold values from -4 to 4
- norm_gain: bfloat16 [7168], replicated, may hold values from 0.099609375 to 1.8984375
- routes: int32 [4096, 8], P(('ctx', 'exp')), may hold values from 0 to 255, as said below
- route_scores: float32 [4096, 8], P(('ctx', 'exp')), may hold values from 0.05 to 1
- w_gate: bfloat16 [16, 7168, 2048], P('exp', None, 'ctx'), may hold values from -0.0625 to 0.0625
- w_up: bfloat16 [16, 7168, 2048], P('exp', None, 'ctx'), may hold values from -0.0625 to 0.0625
- w_down: bfloat16 [16, 2048, 7168], P('exp', 'ctx'), may hold values from -0.125 to 0.125
Outputs:
- attended: bfloat16 [4096, 7168], P(('ctx', 'exp'))
- expert_part: bfloat16 [4096, 7168], P(('ctx', 'exp'))
The draws below stay inside these ranges and needn't reach their ends.
Inputs may be any that keep to these rules, and one draw needn't show every extreme that they name: `routes`: each row names 8 different experts; in the rows of one device no expert in flight is named more than 2 times.
All inputs are finite; a program needn't handle non-finite values.
Results may differ from the reference program's by a relative error of at most 0.035.
Values may be sent and summed in bfloat16 or wider, within the bound.
No kernel may reach another device: no remote copies, remote signals or barrier semaphores. Data moves between devices by JAX's collectives and lax.ppermute only.
A program may use at most 64 MiB of HBM per device.

```python
import math
import jax
import jax.numpy as jnp
from jax import lax

D = 7168
H = 64
LAT = 512
ROPE = 64
VD = 128
FF = 2048
EXPERTS = 256
TOP = 8
BLK = 128
QKW = 576
SEQ = 4096
NBLK = 32
TOK_DEV = 16
CAP = 2
FLIGHT = 16
HEADS_DEV = 4
SLICES = 16
FF_DEV = 128


def draw_latent(key, part):
    key = jax.random.fold_in(key, 3)
    field = jax.random.truncated_normal(key, -8.0, 8.0, (SEQ, QKW), jnp.float32)
    return field.astype(jnp.bfloat16)


def draw_queries(key, part):
    key = jax.random.fold_in(key, 5)
    field = jax.random.truncated_normal(key, -8.0, 8.0, (SEQ, H, QKW), jnp.float32)
    return field.reshape(SEQ, H * QKW).astype(jnp.bfloat16)


def draw_routes(key, part):
    key = jax.random.fold_in(key, 7)
    key_first, key_tail, key_rows, key_other, key_turn = jax.random.split(key, 5)
    per_owner = EXPERTS // FLIGHT
    slots = FLIGHT * CAP
    blocks = SEQ // TOK_DEV
    chosen = jax.random.randint(key_first, (blocks, 1), 0, FLIGHT).astype(jnp.int32)
    listing = (jnp.arange(slots, dtype=jnp.int32)[None, :] + chosen * CAP) % slots // CAP
    tail_perm = jax.vmap(lambda k: jax.random.permutation(k, slots - CAP))(jax.random.split(key_tail, blocks)).astype(jnp.int32)
    tail = jnp.take_along_axis(listing[:, CAP:], tail_perm, axis=1)
    listing = jnp.concatenate([listing[:, :CAP], tail], axis=1)
    if TOK_DEV > slots:
        listing = jnp.concatenate([listing, jnp.full((blocks, TOK_DEV - slots), -1, jnp.int32)], axis=1)
    row_perm = jax.vmap(lambda k: jax.random.permutation(k, TOK_DEV))(jax.random.split(key_rows, blocks)).astype(jnp.int32)
    owner_of = jnp.take_along_axis(listing, row_perm, axis=1).reshape(SEQ)
    numbers = jnp.arange(EXPERTS, dtype=jnp.int32)
    scores = jax.random.randint(key_other, (SEQ, EXPERTS), 0, 2 ** 20).astype(jnp.int32) * EXPERTS + numbers[None, :]
    scores = jnp.where((numbers % per_owner == 0)[None, :], -1, scores)
    picks = lax_top(scores)
    last = jnp.where(owner_of >= 0, owner_of * per_owner, picks[:, TOP - 1])
    lists = jnp.concatenate([picks[:, :TOP - 1], last[:, None]], axis=1)
    turn = jax.random.randint(key_turn, (SEQ, 1), 0, TOP).astype(jnp.int32)
    columns = (jnp.arange(TOP, dtype=jnp.int32)[None, :] + turn) % TOP
    return jnp.take_along_axis(lists, columns, axis=1).astype(jnp.int32)


def lax_top(scores):
    values, picks = jax.lax.top_k(scores, TOP)
    return picks.astype(jnp.int32)


def steps_of(stream_key, dims, shards, smallest, largest):
    level, own = 1.0, jax.random.fold_in(stream_key, 6)
    for position, blocks in shards:
        heights = jnp.exp(jax.random.uniform(jax.random.fold_in(own, position), (blocks,), jnp.float32, smallest / len(shards), largest / len(shards)))
        level = level * jnp.repeat(heights, dims[position] // blocks).reshape([-1 if axis == position else 1 for axis in range(len(dims))])
    return level


def bell_draw(stream_key, dims, spread, reach, shards=(), kind=jnp.bfloat16):
    array = jax.random.normal(stream_key, dims, jnp.float32) * spread
    if len(shards) > 0:
        array = steps_of(stream_key, dims, shards, -0.22, 0.18) * array
    return jnp.clip(array, min=-reach, max=reach).astype(kind)


def setup_inputs(seed: int = 0) -> dict:
    key_of = jax.random.split(jax.random.key(seed), 13)
    return {
        "queries": draw_queries(jax.random.fold_in(key_of[12], 71), 0),
        "latent": draw_latent(jax.random.fold_in(key_of[12], 71), 0),
        "block_order": jax.random.permutation(key_of[2], NBLK).astype(jnp.int32),
        "w_uv": bell_draw(key_of[3], (H, LAT, VD), LAT ** -0.5, 0.25, ((0, 16),)),
        "w_o": bell_draw(key_of[4], (H * VD, D), (H * VD) ** -0.5, 0.0625, ((0, 16), (1, 16))),
        "residual": bell_draw(key_of[5], (SEQ, D), 0.5, 4.0, ((0, 256),)),
        "norm_gain": jnp.clip(1.0 + 0.18 * jax.random.normal(key_of[6], (D,), jnp.float32), 0.099609375, 1.8984375).astype(jnp.bfloat16),
        "routes": draw_routes(jax.random.fold_in(key_of[12], 71), 0),
        "route_scores": jnp.clip(jnp.exp(math.log(1.0) - 2.9957323 * jax.random.uniform(key_of[8], (SEQ, TOP), jnp.float32) ** steps_of(key_of[8], (SEQ, TOP), ((0, 256),), -0.2, 0.2)), 0.05, 1.0),
        "w_gate": bell_draw(key_of[9], (FLIGHT, D, FF), D ** -0.5, 0.0625, ((0, 16), (2, 16))),
        "w_up": bell_draw(key_of[10], (FLIGHT, D, FF), D ** -0.5, 0.0625, ((0, 16), (2, 16))),
        "w_down": bell_draw(key_of[11], (FLIGHT, FF, D), FF ** -0.5, 0.125, ((0, 16), (1, 16))),
    }


def block_places(block_order, count):
    rows = jnp.arange(count, dtype=jnp.int32)
    return block_order[rows // BLK] * BLK + rows % BLK

def rounded(value):
    return lax.optimization_barrier(value.astype(jnp.bfloat16)).astype(jnp.float32)

def reference(queries, latent, block_order, w_uv, w_o, residual, norm_gain, routes, route_scores, w_gate, w_up, w_down):
    place = block_places(block_order, SEQ)
    allowed = place[None, :] <= place[:, None]
    values = latent[:, :LAT]
    scale = (VD + ROPE) ** (-0.5)
    per_head = jnp.swapaxes(queries.reshape(SEQ, H, QKW), 0, 1)

    def one_head(query):
        scores = jnp.dot(query, latent.T, preferred_element_type=jnp.float32) * scale
        scores = jnp.where(allowed, scores, -1e+30)
        highest = lax.optimization_barrier(jnp.max(scores, axis=1, keepdims=True))
        weights = jnp.where(allowed, jnp.exp(scores - highest), 0.0)
        total = lax.optimization_barrier(jnp.sum(weights, axis=1, keepdims=True))
        mixed = jnp.dot(weights.astype(jnp.bfloat16), values, preferred_element_type=jnp.float32)
        return (mixed / total).astype(jnp.bfloat16)
    attn_latent = lax.map(one_head, per_head)
    heads = jnp.einsum('hsl,hlv->shv', attn_latent.astype(jnp.float32), w_uv.astype(jnp.float32)).astype(jnp.bfloat16)
    heads = heads.reshape(SEQ, H * VD)
    width = HEADS_DEV * VD
    running = residual.astype(jnp.float32)
    for group in range(FLIGHT):
        term = jnp.dot(heads[:, group * width:(group + 1) * width], w_o[group * width:(group + 1) * width], preferred_element_type=jnp.float32)
        running = running + rounded(term)
    attended = running.astype(jnp.bfloat16)
    level = attended.astype(jnp.float32)
    normed = (level * lax.rsqrt(lax.optimization_barrier(jnp.mean(level * level, axis=1, keepdims=True)) + 1e-06) * norm_gain.astype(jnp.float32)).astype(jnp.bfloat16)
    share = 2.5 * route_scores / lax.optimization_barrier(jnp.sum(route_scores, axis=1, keepdims=True))
    per_owner = EXPERTS // FLIGHT
    blocks = SEQ // TOK_DEV
    slot_count = blocks * CAP
    token_ids = jnp.arange(SEQ, dtype=jnp.int32)
    combined = jnp.zeros((SEQ, D), jnp.float32)
    for owner in range(FLIGHT):
        match = routes == owner * per_owner
        hits = lax.optimization_barrier(jnp.sum(match.astype(jnp.int32), axis=1))
        weight = lax.optimization_barrier(jnp.sum(jnp.where(match, share, 0.0), axis=1))
        ranking = jnp.cumsum(hits.reshape(blocks, TOK_DEV), axis=1).reshape(SEQ) - 1
        target = jnp.where(hits > 0, token_ids // TOK_DEV * CAP + ranking, slot_count).astype(jnp.int32)
        source = jnp.full((slot_count,), SEQ, jnp.int32).at[target].set(token_ids, mode='drop')
        clipped = jnp.minimum(source, SEQ - 1).astype(jnp.int32)
        picked = normed[clipped]
        gate = jnp.dot(picked, w_gate[owner], preferred_element_type=jnp.float32)
        lifted = jnp.dot(picked, w_up[owner], preferred_element_type=jnp.float32)
        hidden = (jax.nn.silu(gate) * lifted).astype(jnp.bfloat16)
        lowered = jnp.zeros((slot_count, D), jnp.float32)
        for piece in range(SLICES):
            first = piece * FF_DEV
            lowered = lowered + rounded(jnp.dot(hidden[:, first:first + FF_DEV], w_down[owner, first:first + FF_DEV], preferred_element_type=jnp.float32))
        expert_rows = rounded(lowered)
        contribution = jnp.where((source < SEQ)[:, None], expert_rows * weight[clipped][:, None], 0.0)
        combined = combined.at[source].add(contribution, mode='drop')
    return (attended, combined.astype(jnp.bfloat16))
```

```python
import functools
import math

import jax
import jax.numpy as jnp
from jax import lax
from jax.experimental import pallas as pl
from jax.experimental.pallas import tpu as pltpu
from jax.sharding import Mesh, PartitionSpec as P

EXPERTS = 256
BLK = 128
CAP = 2
NZ = 8
CTX = ("z", "xl")
EXP = ("xh", "y", "k")
VMEM_LIMIT = 50 * 2**20


def shift(value, axis, step):
    size = lax.axis_size(axis)
    return lax.ppermute(value, axis, [(i, (i + step) % size) for i in range(size)])


def ring(value):
    found = [None] * NZ
    found[0] = value
    down = up = value
    for step in range(1, NZ // 2):
        down = shift(down, "z", 1)
        up = shift(up, "z", -1)
        found[NZ - step] = down
        found[step] = up
    half = value.shape[0] // 2
    found[NZ // 2] = jnp.concatenate([shift(down[:half], "z", 1), shift(up[half:], "z", -1)], axis=0)
    return found


def attention_kernel(scale, q_ref, near_ref, far_ref, key_place_ref, query_place_ref, w_uv_ref, out_ref):
    heads, width, value_width = w_uv_ref.shape
    rows = q_ref.shape[1]
    part = 256
    parts = near_ref.shape[0] // part
    q = q_ref[0]
    query_place = query_place_ref[0]
    factor = scale * math.log2(math.e)
    highest = jnp.full((rows, 1), -1e30, jnp.float32)
    total = jnp.zeros((rows, 1), jnp.float32)
    mixed = jnp.zeros((rows, width), jnp.float32)
    for index in range(parts):
        scores = []
        newest = highest
        for side, ref in enumerate((near_ref, far_ref)):
            keys = ref[pl.ds(index * part, part), :]
            score = lax.dot_general(q, keys, (((1,), (1,)), ((), ())), preferred_element_type=jnp.float32)
            allowed = key_place_ref[side * parts + index] <= query_place
            score = jnp.where(allowed, score * factor, -1e30)
            newest = jnp.maximum(newest, jnp.max(score, axis=1, keepdims=True))
            scores.append((score, ref))
        shrink = jnp.exp2(highest - newest)
        total = total * shrink
        mixed = mixed * shrink
        for score, ref in scores:
            weights = jnp.exp2(score - newest)
            total = total + jnp.sum(weights, axis=1, keepdims=True)
            values = ref[pl.ds(index * part, part), :width]
            mixed = mixed + jnp.dot(weights.astype(jnp.bfloat16), values, preferred_element_type=jnp.float32)
        highest = newest
    mixed = (mixed / total).astype(jnp.bfloat16)
    tokens = rows // heads
    for head in range(heads):
        out_ref[:, head * value_width : (head + 1) * value_width] = jnp.dot(
            mixed[head * tokens : (head + 1) * tokens], w_uv_ref[head], preferred_element_type=jnp.float32
        ).astype(jnp.bfloat16)


def attention(q, near, far, key_place, query_place, w_uv, scale):
    tiles, rows, key_width = q.shape
    heads, _, value_width = w_uv.shape
    tokens = rows // heads
    whole = pl.BlockSpec(memory_space=pltpu.VMEM)
    return pl.pallas_call(
        functools.partial(attention_kernel, scale),
        grid=(tiles,),
        out_shape=jax.ShapeDtypeStruct((tiles * tokens, heads * value_width), jnp.bfloat16),
        in_specs=[
            pl.BlockSpec((1, rows, key_width), lambda i: (i, 0, 0)),
            whole,
            whole,
            whole,
            pl.BlockSpec((1, rows, 1), lambda i: (i, 0, 0)),
            whole,
        ],
        out_specs=pl.BlockSpec((tokens, heads * value_width), lambda i: (i, 0)),
        compiler_params=pltpu.CompilerParams(vmem_limit_bytes=VMEM_LIMIT),
        name="attention",
    )(q, near, far, key_place, query_place, w_uv)


def project_kernel(a_ref, b_ref, wa_ref, wb_ref, out_ref):
    term = jnp.dot(a_ref[...], wa_ref[0], preferred_element_type=jnp.float32)
    term = term + jnp.dot(b_ref[...], wb_ref[0], preferred_element_type=jnp.float32)
    out_ref[...] = term.astype(jnp.bfloat16).reshape(out_ref.shape)


def project(a, b, wa, wb, group):
    rows, depth = a.shape
    count, _, columns = wa.shape
    whole = pl.BlockSpec((rows, depth), lambda i: (0, 0))
    piece = pl.BlockSpec((1, depth, columns), lambda i: (i, 0, 0))
    return pl.pallas_call(
        project_kernel,
        grid=(count,),
        out_shape=jax.ShapeDtypeStruct((rows // group, count, group, columns), jnp.bfloat16),
        in_specs=[whole, whole, piece, piece],
        out_specs=pl.BlockSpec((rows // group, 1, group, columns), lambda i: (0, i, 0, 0)),
        compiler_params=pltpu.CompilerParams(vmem_limit_bytes=VMEM_LIMIT),
        name="project",
    )(a, b, wa, wb)


def hidden_kernel(x_ref, g0_ref, g1_ref, u0_ref, u1_ref, out_ref, gate, lifted):
    step = pl.program_id(0)

    @pl.when(step == 0)
    def _():
        gate[...] = jnp.zeros_like(gate)
        lifted[...] = jnp.zeros_like(lifted)

    x = x_ref[...]
    gate[...] += jnp.dot(
        x, jnp.concatenate([g0_ref[...], g1_ref[...]], axis=1), preferred_element_type=jnp.float32
    )
    lifted[...] += jnp.dot(
        x, jnp.concatenate([u0_ref[...], u1_ref[...]], axis=1), preferred_element_type=jnp.float32
    )

    @pl.when(step == pl.num_programs(0) - 1)
    def _():
        g = gate[...]
        out_ref[...] = (g / (1.0 + jnp.exp(-g)) * lifted[...]).astype(jnp.bfloat16)


def hidden_units(x, g0, g1, u0, u1):
    rows, depth = x.shape
    width = 2 * g0.shape[1]
    part = 1024
    piece = pl.BlockSpec((part, g0.shape[1]), lambda i: (i, 0))
    return pl.pallas_call(
        hidden_kernel,
        grid=(depth // part,),
        out_shape=jax.ShapeDtypeStruct((rows, width), jnp.bfloat16),
        in_specs=[pl.BlockSpec((rows, part), lambda i: (0, i)), piece, piece, piece, piece],
        out_specs=pl.BlockSpec((rows, width), lambda i: (0, 0)),
        scratch_shapes=[pltpu.VMEM((rows, width), jnp.float32), pltpu.VMEM((rows, width), jnp.float32)],
        compiler_params=pltpu.CompilerParams(vmem_limit_bytes=VMEM_LIMIT),
        name="hidden",
    )(x, g0, g1, u0, u1)


def per_device(
    queries,
    latent,
    block_order,
    w_uv,
    w_o,
    residual,
    norm_gain,
    routes,
    route_scores,
    w_gate,
    w_up,
    w_down,
):
    z = lax.axis_index("z")
    xl = lax.axis_index("xl")
    k = lax.axis_index("k")
    owner_count = 16
    seq_block = queries.shape[0]
    head_count, latent_width, value_width = w_uv.shape
    key_width = latent.shape[1]
    token_count, model_width = residual.shape
    scale = (value_width + key_width - latent_width) ** (-0.5)
    tiles = seq_block // BLK
    column_count = w_o.shape[1]

    own = lax.dynamic_slice_in_dim(latent, k * BLK, BLK, 0)
    other = shift(own, "xl", 1)
    ring_own = ring(own)
    ring_other = ring(other)
    near = jnp.concatenate([v for pair in zip(ring_own, ring_other) for v in pair], axis=0)
    far = shift(near, "k", 1)

    w_o_own = lax.all_gather(w_o, "z", axis=0)
    w_o_other = shift(w_o_own, "k", 1)
    gate_own, lift_own = w_gate[0], w_up[0]
    gate_other = shift(gate_own, "xl", 1)
    lift_other = shift(lift_own, "xl", 1)
    down_width = model_width // NZ
    down_own = []
    for step in range(NZ):
        piece = lax.dynamic_slice_in_dim(w_down[0], lax.rem(z - step + NZ, NZ) * down_width, down_width, 1)
        down_own.append(shift(piece, "z", -step) if step else piece)
    down_own = jnp.stack(down_own)
    down_other = shift(down_own, "xl", 1)

    distance = jnp.arange(NZ, dtype=jnp.int32)[None, :, None]
    turn = jnp.arange(2, dtype=jnp.int32)
    key_block = 2 * (2 * ((z + distance) % NZ) + (xl ^ turn[None, None, :])) + (k ^ turn[:, None, None])
    table = jnp.arange(block_order.shape[0], dtype=jnp.int32)

    def place_of(block):
        pick = block[..., None] == table
        return jnp.sum(jnp.where(pick, block_order, 0), axis=-1) * BLK

    row = jnp.arange(BLK, dtype=jnp.int32)
    key_place = (place_of(key_block)[..., None] + row).reshape(2 * NZ, 1, 2 * BLK)
    query_block = 2 * (2 * z + xl) + jnp.arange(tiles, dtype=jnp.int32)
    query_place = jnp.broadcast_to(
        (place_of(query_block)[:, None] + row)[:, None, :], (tiles, head_count, BLK)
    ).reshape(tiles, head_count * BLK, 1)

    q = queries.reshape(tiles, BLK, head_count, key_width).transpose(0, 2, 1, 3)
    q = q.reshape(tiles, head_count * BLK, key_width)
    heads = attention(q, near, far, key_place, query_place, w_uv, scale)

    heads = heads.reshape(8, 2, token_count, heads.shape[1])
    mine = lax.dynamic_index_in_dim(heads, k, 1, keepdims=False)
    theirs = shift(lax.dynamic_index_in_dim(heads, 1 - k, 1, keepdims=False), "k", 1)
    both = jnp.stack([mine, theirs])
    both_other = shift(both, "xl", 1)
    first = jnp.where(xl == 0, both, both_other)
    second = jnp.where(xl == 0, both_other, both)
    rows = jnp.concatenate([first, second], axis=1).reshape(2, 16 * token_count, -1)
    terms = project(rows[0], rows[1], w_o_own, w_o_other, token_count)
    terms = lax.all_to_all(terms, ("xl", "xh", "y"), split_axis=0, concat_axis=0, tiled=True)
    projected = jnp.sum(terms.reshape(2, 8, NZ, token_count, column_count).astype(jnp.float32), axis=1)
    projected = projected.transpose(2, 1, 0, 3).reshape(token_count, model_width)

    attended = (residual.astype(jnp.float32) + projected).astype(jnp.bfloat16)
    level = attended.astype(jnp.float32)
    normed = (
        level
        * lax.rsqrt(jnp.mean(level * level, axis=1, keepdims=True) + 1e-06)
        * norm_gain.astype(jnp.float32)
    ).astype(jnp.bfloat16)

    share = 2.5 * route_scores / jnp.sum(route_scores, axis=1, keepdims=True)
    chosen = jnp.arange(owner_count, dtype=jnp.int32) * (EXPERTS // owner_count)
    match = routes[:, :, None] == chosen[None, None, :]
    hits = jnp.sum(match.astype(jnp.int32), axis=1)
    weight_to = jnp.sum(jnp.where(match, share[:, :, None], 0.0), axis=1)
    ranking = jnp.cumsum(hits, axis=0) - 1
    slot_ids = jnp.arange(CAP, dtype=jnp.int32)
    select = ((hits[:, :, None] == 1) & (ranking[:, :, None] == slot_ids[None, None, :])).astype(jnp.bfloat16)
    outgoing = jnp.einsum("toc,td->ocd", select, normed, preferred_element_type=jnp.float32).astype(jnp.bfloat16)
    arrived = lax.all_to_all(
        outgoing.reshape(owner_count * CAP, model_width), EXP, split_axis=0, concat_axis=0, tiled=True
    )
    x = jnp.concatenate([a for a in ring(arrived)], axis=0)
    hidden = hidden_units(x, gate_own, gate_other, lift_own, lift_other)
    hidden = jnp.roll(hidden, z * arrived.shape[0], axis=0)
    pieces = ring(hidden)
    units = hidden.shape[1] // 2
    weights = jnp.concatenate([down_own, down_other], axis=1)
    lowered = functools.reduce(
        jnp.add,
        [jnp.dot(pieces[i], weights[i], preferred_element_type=jnp.float32) for i in range(NZ)],
    ).astype(jnp.bfloat16)
    returned = lax.all_to_all(lowered, ("z",) + EXP, split_axis=0, concat_axis=0, tiled=True)
    returned = returned.reshape(NZ, owner_count, CAP, down_width)
    picked = jnp.einsum("toc,zocd->otzd", select, returned, preferred_element_type=jnp.float32)
    picked = picked.reshape(owner_count, token_count, model_width)
    expert_part = jnp.sum(picked * jnp.transpose(weight_to)[:, :, None], axis=0).astype(jnp.bfloat16)
    return (attended, expert_part)


def solution(mesh):
    fine = Mesh(mesh.devices.reshape(NZ, 2, 2, 4, 2), CTX + EXP)
    token = P(CTX + EXP, None)
    return jax.shard_map(
        per_device,
        mesh=fine,
        in_specs=(
            P(CTX, EXP),
            P(CTX, None),
            P(),
            P(EXP, None, None),
            P(EXP, CTX),
            token,
            P(),
            token,
            token,
            P(EXP, None, CTX),
            P(EXP, None, CTX),
            P(EXP, CTX, None),
        ),
        out_specs=(token, token),
        check_vma=False,
    )
```

```python
import functools
import math

import jax
import jax.numpy as jnp
from jax import lax
from jax.experimental import pallas as pl
from jax.experimental.pallas import tpu as pltpu
from jax.sharding import Mesh, PartitionSpec as P

EXPERTS = 256
BLK = 128
CAP = 2
LATENT = 512
PAIR = BLK // 8
WEIGHT_PART = 1024
NZ = 8
CTX = ("z", "xl")
EXP = ("xh", "y", "k")
VMEM_LIMIT = 32 * 2**20


def shift(value, axis, step):
    size = lax.axis_size(axis)
    return lax.ppermute(value, axis, [(i, (i + step) % size) for i in range(size)])


def tie(*values):
    return lax.optimization_barrier(values)


def ring(first, second):
    found = [None] * NZ
    found[0] = (first, second)
    first = ahead = (first, first)
    second = (second, second)
    for step in range(1, NZ // 2):
        first, _ = tie(first, second)
        ahead = (shift(first[0], "z", 1), shift(first[1], "z", -1))
        second, _ = tie(second, first)
        second = (shift(second[0], "z", 1), shift(second[1], "z", -1))
        first = ahead
        found[NZ - step] = (first[0], second[0])
        found[step] = (first[1], second[1])
    found[NZ // 2] = (shift(first[0], "z", 1), shift(second[1], "z", -1))
    return found


def split_kernel(in_ref, out_ref):
    heads = out_ref.shape[1] // in_ref.shape[0]
    tokens, width = in_ref.shape[0], in_ref.shape[1] // heads
    blank = jnp.zeros((tokens, 128 - (width - LATENT)), jnp.bfloat16)
    for head in range(heads):
        value = in_ref[:, head * width : (head + 1) * width]
        tail = value[:, LATENT:]
        rows = slice(head * tokens, (head + 1) * tokens)
        out_ref[0, rows, :LATENT] = value[:, :LATENT]
        out_ref[0, rows, LATENT : LATENT + 128] = jnp.concatenate([tail, blank], axis=1)
        out_ref[0, rows, LATENT + 128 :] = jnp.concatenate([blank, tail], axis=1)


def split_heads(queries, heads):
    rows, columns = queries.shape
    width = LATENT + 256
    return pl.pallas_call(
        split_kernel,
        grid=(rows // BLK,),
        out_shape=jax.ShapeDtypeStruct((rows // BLK, BLK * heads, width), jnp.bfloat16),
        in_specs=[pl.BlockSpec((BLK, columns), lambda i: (i, 0))],
        out_specs=pl.BlockSpec((1, BLK * heads, width), lambda i: (i, 0, 0)),
        compiler_params=pltpu.CompilerParams(vmem_limit_bytes=16 * 2**20),
        name="split",
    )(queries)


def paired(keys):
    half = keys.shape[0] // 2
    return jnp.concatenate(
        [keys[:half, :LATENT], keys[half:, :LATENT], keys[:half, LATENT:], keys[half:, LATENT:]], axis=1
    )


def attention_kernel(scale, groups, first, last, *refs):
    refs = list(refs)
    q_ref = refs.pop(0)
    query_place_ref = refs.pop(0)
    pieces = [[(refs.pop(0), refs.pop(0)) for _ in range(count)] for count in groups]
    factor = scale * math.log2(math.e)
    q = q_ref[0]
    q_first = q[:, : LATENT + 128]
    q_second = jnp.concatenate([q[:, :LATENT], q[:, LATENT + 128 :]], axis=1)
    rows = q.shape[0]
    query_place = query_place_ref[0]
    if first:
        highest = jnp.full((rows, 1), -1e29, jnp.float32)
        total = jnp.zeros((rows, 1), jnp.float32)
        mixed = jnp.zeros((rows, LATENT), jnp.float32)
    else:
        highest_ref, total_ref, mixed_ref = refs.pop(0), refs.pop(0), refs.pop(0)
        highest, total, mixed = highest_ref[0], total_ref[0], mixed_ref[0]
    for group in pieces:
        scores = []
        newest = highest
        for key_ref, place_ref in group:
            first_keys = jnp.concatenate([key_ref[:, :LATENT], key_ref[:, 2 * LATENT :]], axis=1)
            second_keys = key_ref[:, LATENT:]
            for keys, queries, offset in ((first_keys, q_first, 0), (second_keys, q_second, PAIR)):
                score = lax.dot_general(
                    queries, keys, (((1,), (1,)), ((), ())), preferred_element_type=jnp.float32
                )
                score = jnp.where(place_ref[...] + offset <= query_place, score * factor, -1e30)
                newest = jnp.maximum(newest, jnp.max(score, axis=1, keepdims=True))
                scores.append((score, key_ref, 0 if offset == 0 else LATENT))
        shrink = jnp.exp2(highest - newest)
        total = total * shrink
        mixed = mixed * shrink
        for score, key_ref, start in scores:
            weights = jnp.exp2(score - newest)
            total = total + jnp.sum(weights, axis=1, keepdims=True)
            mixed = mixed + jnp.dot(
                weights.astype(jnp.bfloat16),
                key_ref[:, start : start + LATENT],
                preferred_element_type=jnp.float32,
            )
        highest = newest
    if not last:
        highest_ref, total_ref, mixed_ref = refs
        highest_ref[0], total_ref[0], mixed_ref[0] = highest, total, mixed
        return
    w_uv_ref, out_ref = refs
    heads, _, value_width = w_uv_ref.shape
    mixed = (mixed / total).astype(jnp.bfloat16)
    tokens = rows // heads
    for head in range(heads):
        out_ref[:, head * value_width : (head + 1) * value_width] = jnp.dot(
            mixed[head * tokens : (head + 1) * tokens], w_uv_ref[head], preferred_element_type=jnp.float32
        ).astype(jnp.bfloat16)


def attention(q, query_place, groups, state, w_uv, scale):
    tiles, rows, key_width = q.shape
    whole = pl.BlockSpec(memory_space=pltpu.VMEM)
    tile = lambda *shape: pl.BlockSpec((1,) + shape, lambda i: (i,) + (0,) * len(shape))
    narrow, wide = tile(rows, 1), tile(rows, LATENT)
    flat = [v for group in groups for pair in group for v in pair]
    operands = [q, query_place] + flat
    specs = [tile(rows, key_width), narrow] + [whole] * len(flat)
    if state:
        operands += state
        specs += [narrow, narrow, wide]
    if w_uv is None:
        out_shape = [
            jax.ShapeDtypeStruct((tiles, rows, 1), jnp.float32),
            jax.ShapeDtypeStruct((tiles, rows, 1), jnp.float32),
            jax.ShapeDtypeStruct((tiles, rows, LATENT), jnp.float32),
        ]
        out_specs = [narrow, narrow, wide]
    else:
        heads, _, value_width = w_uv.shape
        operands.append(w_uv)
        specs.append(whole)
        out_shape = jax.ShapeDtypeStruct((tiles * rows // heads, heads * value_width), jnp.bfloat16)
        out_specs = pl.BlockSpec((rows // heads, heads * value_width), lambda i: (i, 0))
    keys = sum(pair[0].shape[0] for group in groups for pair in group)
    return pl.pallas_call(
        functools.partial(
            attention_kernel, scale, tuple(len(g) for g in groups), not state, w_uv is not None
        ),
        grid=(tiles,),
        out_shape=out_shape,
        in_specs=specs,
        out_specs=out_specs,
        compiler_params=pltpu.CompilerParams(vmem_limit_bytes=VMEM_LIMIT),
        name="attention",
    )(*operands)


def project_kernel(a_ref, b_ref, wa_ref, wb_ref, out_ref):
    against = (((1,), (1,)), ((), ()))
    depth = a_ref.shape[1]
    term = lax.dot_general(
        a_ref[...], wa_ref[...].reshape(-1, depth), against, preferred_element_type=jnp.float32
    )
    term = term + lax.dot_general(
        b_ref[...], wb_ref[...].reshape(-1, depth), against, preferred_element_type=jnp.float32
    )
    out_ref[...] = term.astype(jnp.bfloat16).reshape(out_ref.shape)


def project(a, b, wa, wb, group):
    rows, depth = a.shape
    count, columns, _ = wa.shape
    whole = pl.BlockSpec((rows, depth), lambda i: (0, 0))
    piece = pl.BlockSpec((2, columns, depth), lambda i: (i, 0, 0))
    return pl.pallas_call(
        project_kernel,
        grid=(count // 2,),
        out_shape=jax.ShapeDtypeStruct((rows // group, count // 2, group, 2 * columns), jnp.bfloat16),
        in_specs=[whole, whole, piece, piece],
        out_specs=pl.BlockSpec((rows // group, 1, group, 2 * columns), lambda i: (0, i, 0, 0)),
        compiler_params=pltpu.CompilerParams(vmem_limit_bytes=16 * 2**20),
        name="project",
    )(a, b, wa, wb)


def hidden_kernel(starts, *refs):
    *refs, out_ref, gate, lifted = refs
    count = len(starts)
    *x_refs, gate_ref, lift_ref = refs[: -2 * count]
    step = pl.program_id(0)

    @pl.when(step == 0)
    def _():
        gate[...] = jnp.zeros_like(gate)
        lifted[...] = jnp.zeros_like(lifted)

    x = jnp.concatenate([ref[...] for ref in x_refs], axis=0)
    for total, own_ref, others in (
        (gate, gate_ref, refs[-2 * count : -count]),
        (lifted, lift_ref, refs[-count:]),
    ):
        other = others[0][...]
        for start, ref in zip(starts[1:], others[1:]):
            other = jnp.where(step < start, other, ref[...])
        weights = jnp.concatenate([own_ref[...], other], axis=1)
        total[...] += jnp.dot(x, weights, preferred_element_type=jnp.float32)

    @pl.when(step == pl.num_programs(0) - 1)
    def _():
        g = gate[...]
        out_ref[...] = (g / (1.0 + jnp.exp(-g)) * lifted[...]).astype(jnp.bfloat16)


def hidden_units(xs, gate_own, lift_own, gate_others, lift_others):
    rows, depth = sum(x.shape[0] for x in xs), xs[0].shape[1]
    units = gate_own.shape[1]
    starts = [0]
    for piece in gate_others[:-1]:
        starts.append(starts[-1] + piece.shape[0] // WEIGHT_PART)

    def at(start, piece):
        last = piece.shape[0] // WEIGHT_PART - 1
        return pl.BlockSpec((WEIGHT_PART, units), lambda i: (jnp.clip(i - start, 0, last), 0))

    own = pl.BlockSpec((WEIGHT_PART, units), lambda i: (i, 0))
    others = [at(s, p) for s, p in zip(starts, gate_others)]
    return pl.pallas_call(
        functools.partial(hidden_kernel, tuple(starts)),
        grid=(depth // WEIGHT_PART,),
        out_shape=jax.ShapeDtypeStruct((rows, 2 * units), jnp.bfloat16),
        in_specs=[pl.BlockSpec((x.shape[0], WEIGHT_PART), lambda i: (0, i)) for x in xs]
        + [own, own]
        + others
        + others,
        out_specs=pl.BlockSpec((rows, 2 * units), lambda i: (0, 0)),
        scratch_shapes=[pltpu.VMEM((rows, 2 * units), jnp.float32)] * 2,
        compiler_params=pltpu.CompilerParams(vmem_limit_bytes=60 * 2**20),
        name="hidden",
    )(*xs, gate_own, lift_own, *gate_others, *lift_others)


def pack_kernel(*refs):
    *in_refs, out_ref = refs
    for i, ref in enumerate(in_refs):
        out_ref[i] = ref[...]


def pack(pieces):
    whole = pl.BlockSpec(memory_space=pltpu.VMEM)
    return pl.pallas_call(
        pack_kernel,
        out_shape=jax.ShapeDtypeStruct((len(pieces),) + pieces[0].shape, pieces[0].dtype),
        in_specs=[whole] * len(pieces),
        out_specs=whole,
        compiler_params=pltpu.CompilerParams(vmem_limit_bytes=16 * 2**20),
        name="pack",
    )(*pieces)


def lower_kernel(hidden_ref, own_ref, other_ref, out_ref):
    units = own_ref.shape[0]
    total = jnp.dot(hidden_ref[:, :units], own_ref[...], preferred_element_type=jnp.float32)
    total = total + jnp.dot(hidden_ref[:, units:], other_ref[...], preferred_element_type=jnp.float32)
    out_ref[...] = total.astype(jnp.bfloat16)


def lower(hidden, own, other):
    rows, width = hidden.shape
    units, columns = own.shape
    part = 512
    piece = pl.BlockSpec((units, part), lambda i: (0, i))
    return pl.pallas_call(
        lower_kernel,
        grid=(columns // part,),
        out_shape=jax.ShapeDtypeStruct((rows, columns), jnp.bfloat16),
        in_specs=[pl.BlockSpec((rows, width), lambda i: (0, 0)), piece, piece],
        out_specs=pl.BlockSpec((rows, part), lambda i: (0, i)),
        compiler_params=pltpu.CompilerParams(vmem_limit_bytes=16 * 2**20),
        name="lower",
    )(hidden, own, other)


def per_device(
    queries,
    latent,
    block_order,
    w_uv,
    w_o,
    residual,
    norm_gain,
    routes,
    route_scores,
    w_gate,
    w_up,
    w_down,
):
    z = lax.axis_index("z")
    xl = lax.axis_index("xl")
    y = lax.axis_index("y")
    k = lax.axis_index("k")
    owner_count = 16
    seq_block = queries.shape[0]
    head_count, latent_width, value_width = w_uv.shape
    key_width = latent.shape[1]
    token_count, model_width = residual.shape
    scale = (value_width + key_width - latent_width) ** (-0.5)
    tiles = seq_block // BLK
    column_count = w_o.shape[1]

    part = BLK // 4
    own = lax.dynamic_slice_in_dim(latent, k * BLK + y * part, part, 0)
    own = paired(own)
    other = shift(own, "xl", 1)
    gate_own, lift_own = w_gate[0], w_up[0]
    early = 4 * WEIGHT_PART
    pair = jnp.concatenate([own, other], axis=0)
    pair, gate_sent, lift_sent = tie(pair, gate_own, lift_own)
    gate_others = [shift(v, "xl", 1) for v in (gate_sent[:early], gate_sent[early:])]
    lift_others = [shift(lift_sent[:early], "xl", 1)]
    down = up = pair
    found = [pair]
    for _ in range(1, NZ // 2):
        down, up = shift(down, "z", 1), shift(up, "z", -1)
        found = [down] + found + [up]
    down, up = shift(down[:PAIR], "z", 1), shift(up[PAIR:], "z", -1)
    near = pack(found + [jnp.concatenate([down, up], axis=0)]).reshape(-1, pair.shape[1])
    near, w_o, gate_others[0] = tie(near, w_o, gate_others[0])
    w_o_own = lax.all_gather(w_o.T, "z", axis=0)

    turn = jnp.arange(2, dtype=jnp.int32)
    where = (z + jnp.arange(1 - NZ // 2, NZ // 2 + 1, dtype=jnp.int32)) % NZ
    key_block = 2 * (2 * where[:, None] + (xl ^ turn)) + (k ^ turn[:, None, None])
    table = jnp.arange(block_order.shape[0], dtype=jnp.int32)

    def place_of(block):
        pick = block[..., None] == table
        return jnp.sum(jnp.where(pick, block_order, 0), axis=-1) * BLK

    row = jnp.arange(BLK, dtype=jnp.int32)
    key_place = place_of(key_block) + ((y + jnp.arange(4, dtype=jnp.int32)) % 4 * part)[
        :, None, None, None
    ]
    key_place = (key_place[..., None] + row[:PAIR]).reshape(4, 2, 1, -1)
    query_block = 2 * (2 * z + xl) + jnp.arange(tiles, dtype=jnp.int32)
    query_place = jnp.broadcast_to(
        (place_of(query_block)[:, None] + row)[:, None, :], (tiles, head_count, BLK)
    ).reshape(tiles, head_count * BLK, 1)

    q = split_heads(queries, head_count)

    def both_cores(keys, distance, first=None, last=None):
        return [
            (keys, key_place[distance, 0, :, first:last]),
            (shift(keys, "k", 1), key_place[distance, 1, :, first:last]),
        ]

    half = near.shape[0] // 2
    down, up = shift(near, "y", 1), shift(near, "y", -1)
    state = attention(q, query_place, [both_cores(near, 0)], None, None, scale)
    down, up, gate_others[1], *state = tie(down, up, gate_others[1], *state)
    across = shift(down[:half], "y", 1), shift(up[half:], "y", -1)
    state = attention(q, query_place, [both_cores(up, 1), both_cores(down, 3)], state, None, scale)
    *across, state = tie(*across, state)
    groups = [both_cores(across[0], 2, None, half) + both_cores(across[1], 2, half, None)]
    heads = attention(q, query_place, groups, state, w_uv, scale)
    w_o_own, w_down = tie(w_o_own, w_down)
    down_width = model_width // NZ
    down_pieces = []
    for step in range(NZ):
        piece = lax.dynamic_slice_in_dim(w_down[0], lax.rem(z - step + NZ, NZ) * down_width, down_width, 1)
        down_pieces.append(shift(piece, "z", -step) if step else piece)

    heads, w_o_own, lift_others[0] = tie(heads, w_o_own, lift_others[0])
    w_o_other = shift(w_o_own, "k", 1)

    heads = heads.reshape(8, 2, token_count, heads.shape[1])
    mine = lax.dynamic_index_in_dim(heads, k, 1, keepdims=False)
    theirs = shift(lax.dynamic_index_in_dim(heads, 1 - k, 1, keepdims=False), "k", 1)
    both = jnp.stack([mine, theirs])
    both_other = shift(both, "xl", 1)
    first = jnp.where(xl == 0, both, both_other)
    second = jnp.where(xl == 0, both_other, both)
    rows = jnp.concatenate([first, second], axis=1).reshape(2, 16 * token_count, -1)
    terms = project(rows[0], rows[1], w_o_own, w_o_other, token_count)
    terms = lax.all_to_all(terms, ("xl", "xh", "y"), split_axis=0, concat_axis=0, tiled=True)
    projected = jnp.sum(terms.reshape((2, 8) + terms.shape[1:]).astype(jnp.float32), axis=1)
    projected = projected.reshape(2, NZ // 2, token_count, 2, column_count)
    projected = projected.transpose(2, 1, 3, 0, 4).reshape(token_count, model_width)

    attended = (residual.astype(jnp.float32) + projected).astype(jnp.bfloat16)
    level = attended.astype(jnp.float32)
    normed = (
        level
        * lax.rsqrt(jnp.mean(level * level, axis=1, keepdims=True) + 1e-06)
        * norm_gain.astype(jnp.float32)
    ).astype(jnp.bfloat16)

    share = 2.5 * route_scores / jnp.sum(route_scores, axis=1, keepdims=True)
    chosen = jnp.arange(owner_count, dtype=jnp.int32) * (EXPERTS // owner_count)
    match = routes[:, :, None] == chosen[None, None, :]
    hits = jnp.sum(match.astype(jnp.int32), axis=1)
    weight_to = jnp.sum(jnp.where(match, share[:, :, None], 0.0), axis=1)
    ranking = jnp.cumsum(hits, axis=0) - 1
    slot_ids = jnp.arange(CAP, dtype=jnp.int32)
    select = ((hits[:, :, None] == 1) & (ranking[:, :, None] == slot_ids[None, None, :])).astype(jnp.bfloat16)
    outgoing = jnp.einsum("toc,td->ocd", select, normed, preferred_element_type=jnp.float32).astype(jnp.bfloat16)
    arrived = lax.all_to_all(
        outgoing.reshape(owner_count * CAP, model_width), EXP, split_axis=0, concat_axis=0, tiled=True
    )
    arrived, lift_rest, w_down = tie(arrived, lift_own[early:], w_down[0])
    lift_others.append(shift(lift_rest, "xl", 1))
    columns = model_width // 2
    down_own = lax.dynamic_slice_in_dim(w_down, xl * columns, columns, 1)
    down_sent = lax.dynamic_slice_in_dim(w_down, (1 - xl) * columns, columns, 1)
    down_other = shift(down_sent, "xl", 1)
    half = arrived.shape[0] // 2
    xs = [v for pair in ring(arrived[:half], arrived[half:]) for v in pair]
    hidden = hidden_units(xs, gate_own, lift_own, gate_others, lift_others)
    hidden = jnp.roll(hidden, z * arrived.shape[0], axis=0)
    units = hidden.shape[1] // 2
    theirs = shift(hidden, "xl", 1)
    theirs = jnp.concatenate([theirs[:, units:], theirs[:, :units]], axis=1)
    hidden, theirs = (v.reshape(NZ, 1, -1, 2 * units) for v in (hidden, theirs))
    hidden = jnp.where(
        xl == 0, jnp.concatenate([hidden, theirs], axis=1), jnp.concatenate([theirs, hidden], axis=1)
    ).reshape(-1, 2 * units)
    lowered = lax.psum_scatter(
        lower(hidden, down_own, down_other), "z", scatter_dimension=0, tiled=True
    )
    returned = lax.all_to_all(lowered, ("xl",) + EXP, split_axis=0, concat_axis=0, tiled=True)
    returned = returned.reshape(2, owner_count, CAP, columns)
    picked = jnp.einsum("toc,xocd->otxd", select, returned, preferred_element_type=jnp.float32)
    picked = picked.reshape(owner_count, token_count, model_width)
    expert_part = jnp.sum(picked * jnp.transpose(weight_to)[:, :, None], axis=0).astype(jnp.bfloat16)
    return (attended, expert_part)


def solution(mesh):
    fine = Mesh(mesh.devices.reshape(NZ, 2, 2, 4, 2), CTX + EXP)
    token = P(CTX + EXP, None)
    return jax.shard_map(
        per_device,
        mesh=fine,
        in_specs=(
            P(CTX, EXP),
            P(CTX, None),
            P(),
            P(EXP, None, None),
            P(EXP, CTX),
            token,
            P(),
            token,
            token,
            P(EXP, None, CTX),
            P(EXP, None, CTX),
            P(EXP, CTX, None),
        ),
        out_specs=(token, token),
        check_vma=False,
    )
```

```python
import functools
import math

import jax
import jax.numpy as jnp
from jax import lax
from jax.experimental import pallas as pl
from jax.experimental.pallas import tpu as pltpu
from jax.sharding import Mesh, PartitionSpec as P

EXPERTS = 256
BLK = 128
CAP = 2
LATENT = 512
PAIR = BLK // 8
WEIGHT_PART = 1024
NZ = 8
CTX = ("z", "xl")
EXP = ("xh", "y", "k")
VMEM_LIMIT = 20 * 2**20


def shift(value, axis, step):
    size = lax.axis_size(axis)
    return lax.ppermute(value, axis, [(i, (i + step) % size) for i in range(size)])


def tie(*values):
    return lax.optimization_barrier(values)


def with_some(value, pieces, steps):
    value, *ready = tie(value, *(pieces[s] for s in steps))
    pieces.update(zip(steps, ready))
    return value


def block_of(shape):
    return pl.BlockSpec(shape, lambda *_: (0,) * len(shape))


def split_kernel(in_ref, out_ref):
    heads = out_ref.shape[1] // in_ref.shape[0]
    tokens, width = in_ref.shape[0], in_ref.shape[1] // heads
    blank = jnp.zeros((tokens, 128 - (width - LATENT)), jnp.bfloat16)
    for head in range(heads):
        value = in_ref[:, head * width : (head + 1) * width]
        tail = value[:, LATENT:]
        rows = slice(head * tokens, (head + 1) * tokens)
        out_ref[0, rows, :LATENT] = value[:, :LATENT]
        out_ref[0, rows, LATENT : LATENT + 128] = jnp.concatenate([tail, blank], axis=1)
        out_ref[0, rows, LATENT + 128 :] = jnp.concatenate([blank, tail], axis=1)


def split_heads(queries, heads):
    rows, columns = queries.shape
    width = LATENT + 256
    return pl.pallas_call(
        split_kernel,
        grid=(rows // BLK,),
        out_shape=jax.ShapeDtypeStruct((rows // BLK, BLK * heads, width), jnp.bfloat16),
        in_specs=[pl.BlockSpec((BLK, columns), lambda i: (i, 0))],
        out_specs=pl.BlockSpec((1, BLK * heads, width), lambda i: (i, 0, 0)),
        compiler_params=pltpu.CompilerParams(vmem_limit_bytes=16 * 2**20),
        name="split",
    )(queries)


def paired(keys):
    half = keys.shape[0] // 2
    return jnp.concatenate(
        [keys[:half, :LATENT], keys[half:, :LATENT], keys[:half, LATENT:], keys[half:, LATENT:]], axis=1
    )


def attention_kernel(scale, groups, first, last, *refs):
    refs = list(refs)
    q_ref = refs.pop(0)
    query_place_ref = refs.pop(0)
    pieces = [[(refs.pop(0), refs.pop(0)) for _ in range(count)] for count in groups]
    factor = scale * math.log2(math.e)
    q = q_ref[0]
    q_first = q[:, : LATENT + 128]
    q_second = jnp.concatenate([q[:, :LATENT], q[:, LATENT + 128 :]], axis=1)
    rows = q.shape[0]
    query_place = query_place_ref[0]
    if first:
        highest = jnp.full((rows, 1), -1e29, jnp.float32)
        total = jnp.zeros((rows, 1), jnp.float32)
        mixed = jnp.zeros((rows, LATENT), jnp.float32)
    else:
        highest_ref, total_ref, mixed_ref = refs.pop(0), refs.pop(0), refs.pop(0)
        highest, total, mixed = highest_ref[0], total_ref[0], mixed_ref[0]
    for group in pieces:
        scores = []
        newest = highest
        for key_ref, place_ref in group:
            first_keys = jnp.concatenate([key_ref[:, :LATENT], key_ref[:, 2 * LATENT :]], axis=1)
            second_keys = key_ref[:, LATENT:]
            for keys, queries, offset in ((first_keys, q_first, 0), (second_keys, q_second, PAIR)):
                score = lax.dot_general(
                    queries, keys, (((1,), (1,)), ((), ())), preferred_element_type=jnp.float32
                )
                score = jnp.where(place_ref[...] + offset <= query_place, score * factor, -1e30)
                newest = jnp.maximum(newest, jnp.max(score, axis=1, keepdims=True))
                scores.append((score, key_ref, 0 if offset == 0 else LATENT))
        shrink = jnp.exp2(highest - newest)
        total = total * shrink
        mixed = mixed * shrink
        for score, key_ref, start in scores:
            weights = jnp.exp2(score - newest)
            total = total + jnp.sum(weights, axis=1, keepdims=True)
            mixed = mixed + jnp.dot(
                weights.astype(jnp.bfloat16),
                key_ref[:, start : start + LATENT],
                preferred_element_type=jnp.float32,
            )
        highest = newest
    if not last:
        highest_ref, total_ref, mixed_ref = refs
        highest_ref[0], total_ref[0], mixed_ref[0] = highest, total, mixed
        return
    w_uv_ref, out_ref = refs
    heads, _, value_width = w_uv_ref.shape
    mixed = (mixed / total).astype(jnp.bfloat16)
    tokens = rows // heads
    for head in range(heads):
        out_ref[:, head * value_width : (head + 1) * value_width] = jnp.dot(
            mixed[head * tokens : (head + 1) * tokens], w_uv_ref[head], preferred_element_type=jnp.float32
        ).astype(jnp.bfloat16)


def attention(q, query_place, groups, state, w_uv, scale):
    tiles, rows, key_width = q.shape
    whole = pl.BlockSpec(memory_space=pltpu.VMEM)
    tile = lambda *shape: pl.BlockSpec((1,) + shape, lambda i: (i,) + (0,) * len(shape))
    narrow, wide = tile(rows, 1), tile(rows, LATENT)
    flat = [v for group in groups for pair in group for v in pair]
    operands = [q, query_place] + flat
    specs = [tile(rows, key_width), narrow] + [whole] * len(flat)
    if state:
        operands += state
        specs += [narrow, narrow, wide]
    if w_uv is None:
        out_shape = [
            jax.ShapeDtypeStruct((tiles, rows, 1), jnp.float32),
            jax.ShapeDtypeStruct((tiles, rows, 1), jnp.float32),
            jax.ShapeDtypeStruct((tiles, rows, LATENT), jnp.float32),
        ]
        out_specs = [narrow, narrow, wide]
    else:
        heads, _, value_width = w_uv.shape
        operands.append(w_uv)
        specs.append(whole)
        out_shape = jax.ShapeDtypeStruct((tiles * rows // heads, heads * value_width), jnp.bfloat16)
        out_specs = pl.BlockSpec((rows // heads, heads * value_width), lambda i: (i, 0))
    keys = 2 * sum(pair[0].shape[0] for group in groups for pair in group)
    return pl.pallas_call(
        functools.partial(
            attention_kernel, scale, tuple(len(g) for g in groups), not state, w_uv is not None
        ),
        grid=(tiles,),
        out_shape=out_shape,
        in_specs=specs,
        out_specs=out_specs,
        compiler_params=pltpu.CompilerParams(vmem_limit_bytes=VMEM_LIMIT),
        name="attention",
    )(*operands)


def project_kernel(a_ref, b_ref, wa_ref, wb_ref, out_ref, held_a, held_b, sems):
    steps = out_ref.shape[1]
    copies = []
    for i in range(steps):
        pair = pl.ds(2 * i, 2)
        copies.append(
            (
                pltpu.make_async_copy(wa_ref.at[pair], held_a.at[pair], sems.at[0, i]),
                pltpu.make_async_copy(wb_ref.at[pair], held_b.at[pair], sems.at[1, i]),
            )
        )
        for copy in copies[-1]:
            copy.start()
    against = (((1,), (1,)), ((), ()))
    depth = a_ref.shape[1]
    for i in range(steps):
        term = 0.0
        for copy, held, ref in zip(copies[i], (held_a, held_b), (a_ref, b_ref)):
            copy.wait()
            term = term + lax.dot_general(
                ref[...], held[2 * i : 2 * i + 2].reshape(-1, depth), against, preferred_element_type=jnp.float32
            )
        groups, _, rows, columns = out_ref.shape
        out_ref[:, i] = term.astype(jnp.bfloat16).reshape(groups, rows, columns)


def project(a, b, wa, wb, group):
    rows, depth = a.shape
    count, columns, _ = wa.shape
    out = (rows // group, count // 2, group, 2 * columns)
    anywhere = pl.BlockSpec(memory_space=pl.ANY)
    return pl.pallas_call(
        project_kernel,
        grid=(1,),
        out_shape=jax.ShapeDtypeStruct(out, jnp.bfloat16),
        in_specs=[block_of(a.shape), block_of(b.shape), anywhere, anywhere],
        out_specs=block_of(out),
        scratch_shapes=[pltpu.VMEM(wa.shape, jnp.bfloat16)] * 2
        + [pltpu.SemaphoreType.DMA((2, count // 2))],
        compiler_params=pltpu.CompilerParams(vmem_limit_bytes=60 * 2**20),
        name="project",
    )(a, b, wa, wb)


def hidden_kernel(counts, *refs):
    *refs, out_ref, held, w_held, x_sems, w_sems = refs
    x_refs, refs = refs[: -sum(counts)], refs[-sum(counts) :]
    rows = x_refs[0].shape[0]
    x_copies = [
        pltpu.make_async_copy(ref, held.at[pl.ds(i * rows, rows)], x_sems.at[i]) for i, ref in enumerate(x_refs)
    ]
    for copy in x_copies:
        copy.start()
    steps = w_held.shape[1] // WEIGHT_PART
    copies = []
    for which, count in enumerate(counts):
        pieces, refs = refs[:count], refs[count:]
        at = 0
        for ref in pieces:
            for start in range(0, ref.shape[0], WEIGHT_PART):
                copies.append(
                    (
                        at,
                        pltpu.make_async_copy(
                            ref.at[pl.ds(start, WEIGHT_PART)],
                            w_held.at[which, pl.ds(at * WEIGHT_PART, WEIGHT_PART)],
                            w_sems.at[which, at],
                        ),
                    )
                )
                at += 1
    copies.sort(key=lambda pair: pair[0])
    for _, copy in copies:
        copy.start()
    for copy in x_copies:
        copy.wait()
    gate = lifted = 0.0
    for step in range(steps):
        for at, copy in copies:
            if at == step:
                copy.wait()
        part = slice(step * WEIGHT_PART, (step + 1) * WEIGHT_PART)
        x = held[:, part]
        gate = gate + jnp.dot(
            x, jnp.concatenate([w_held[0, part], w_held[1, part]], axis=1), preferred_element_type=jnp.float32
        )
        lifted = lifted + jnp.dot(
            x, jnp.concatenate([w_held[2, part], w_held[3, part]], axis=1), preferred_element_type=jnp.float32
        )
    out_ref[...] = (gate / (1.0 + jnp.exp(-gate)) * lifted).astype(jnp.bfloat16)


def hidden_units(xs, gate_own, lift_own, gate_others, lift_others):
    rows, depth = sum(x.shape[0] for x in xs), xs[0].shape[1]
    units = gate_own.shape[1]
    pieces = [[gate_own], gate_others, [lift_own], lift_others]
    flat = [v for group in pieces for v in group]
    return pl.pallas_call(
        functools.partial(hidden_kernel, tuple(len(group) for group in pieces)),
        grid=(1,),
        out_shape=jax.ShapeDtypeStruct((rows, 2 * units), jnp.bfloat16),
        in_specs=[pl.BlockSpec(memory_space=pl.ANY)] * (len(xs) + len(flat)),
        out_specs=block_of((rows, 2 * units)),
        scratch_shapes=[
            pltpu.VMEM((rows, depth), jnp.bfloat16),
            pltpu.VMEM((4, depth, units), jnp.bfloat16),
            pltpu.SemaphoreType.DMA((len(xs),)),
            pltpu.SemaphoreType.DMA((4, depth // WEIGHT_PART)),
        ],
        compiler_params=pltpu.CompilerParams(vmem_limit_bytes=60 * 2**20),
        name="hidden",
    )(*xs, *flat)


def pack_kernel(*refs):
    *in_refs, out_ref = refs
    for i, ref in enumerate(in_refs):
        out_ref[i] = ref[...]


def pack(pieces):
    whole = pl.BlockSpec(memory_space=pltpu.VMEM)
    return pl.pallas_call(
        pack_kernel,
        out_shape=jax.ShapeDtypeStruct((len(pieces),) + pieces[0].shape, pieces[0].dtype),
        in_specs=[whole] * len(pieces),
        out_specs=whole,
        compiler_params=pltpu.CompilerParams(vmem_limit_bytes=16 * 2**20),
        name="pack",
    )(*pieces)


def lower_kernel(*refs):
    *hidden_refs, own_ref, other_ref, out_ref = refs
    units = own_ref.shape[1]
    total = jnp.zeros(out_ref.shape, jnp.float32)
    for step in range(NZ):
        at = step
        piece = hidden_refs[step][...] if step < NZ // 2 else hidden_refs[step + 1][...]
        if step == NZ // 2:
            piece = jnp.concatenate([hidden_refs[step][...], piece], axis=0)
        total = total + jnp.dot(piece[:, :units], own_ref[at], preferred_element_type=jnp.float32)
        total = total + jnp.dot(piece[:, units:], other_ref[at], preferred_element_type=jnp.float32)
    out_ref[...] = total.astype(jnp.bfloat16)


def lower(pieces, own, other):
    rows = pieces[0].shape[0]
    columns = own.shape[2]
    whole = pl.BlockSpec(memory_space=pltpu.VMEM)
    return pl.pallas_call(
        lower_kernel,
        out_shape=jax.ShapeDtypeStruct((rows, columns), jnp.bfloat16),
        in_specs=[whole] * (len(pieces) + 2),
        out_specs=whole,
        compiler_params=pltpu.CompilerParams(vmem_limit_bytes=16 * 2**20),
        name="lower",
    )(*pieces, own, other)


def per_device(
    queries,
    latent,
    block_order,
    w_uv,
    w_o,
    residual,
    norm_gain,
    routes,
    route_scores,
    w_gate,
    w_up,
    w_down,
):
    z = lax.axis_index("z")
    xl = lax.axis_index("xl")
    y = lax.axis_index("y")
    k = lax.axis_index("k")
    owner_count = 16
    seq_block = queries.shape[0]
    head_count, latent_width, value_width = w_uv.shape
    key_width = latent.shape[1]
    token_count, model_width = residual.shape
    scale = (value_width + key_width - latent_width) ** (-0.5)
    tiles = seq_block // BLK
    column_count = w_o.shape[1]

    part = BLK // 4
    own = lax.dynamic_slice_in_dim(latent, k * BLK + y * part, part, 0)
    own = paired(own)
    other = shift(own, "xl", 1)
    gate_own, lift_own = w_gate[0], w_up[0]
    early = 3 * WEIGHT_PART
    pair = jnp.concatenate([own, other], axis=0)
    pair, gate_sent, lift_sent, w_o = tie(pair, gate_own, lift_own, w_o)
    cuts = [0, 4 * WEIGHT_PART, 6 * WEIGHT_PART, gate_sent.shape[0]]
    gate_others = [shift(gate_sent[i:j], "xl", 1) for i, j in zip(cuts, cuts[1:])]
    w_o_own = lax.all_gather(w_o.T, "z", axis=0)
    down, down2, up, up2 = (shift(pair, "z", s) for s in (1, 2, -1, -2))
    down3, up3 = shift(down2, "z", 1), shift(up2, "z", -1)
    far = jnp.concatenate([shift(down2[:PAIR], "z", 2), shift(up2[PAIR:], "z", -2)], axis=0)
    near = pack([down3, down2, down, pair, up, up2, up3, far]).reshape(-1, pair.shape[1])
    near, lift_sent, gate_others[0] = tie(near, lift_sent, gate_others[0])
    lift_others = [shift(lift_sent[:early], "xl", 1)]

    turn = jnp.arange(2, dtype=jnp.int32)
    where = (z + jnp.arange(1 - NZ // 2, NZ // 2 + 1, dtype=jnp.int32)) % NZ
    key_block = 2 * (2 * where[:, None] + (xl ^ turn)) + (k ^ turn[:, None, None])
    table = jnp.arange(block_order.shape[0], dtype=jnp.int32)

    def place_of(block):
        pick = block[..., None] == table
        return jnp.sum(jnp.where(pick, block_order, 0), axis=-1) * BLK

    row = jnp.arange(BLK, dtype=jnp.int32)
    key_place = place_of(key_block) + ((y + jnp.arange(4, dtype=jnp.int32)) % 4 * part)[
        :, None, None, None
    ]
    key_place = (key_place[..., None] + row[:PAIR]).reshape(4, 2, 1, -1)
    query_block = 2 * (2 * z + xl) + jnp.arange(tiles, dtype=jnp.int32)
    query_place = jnp.broadcast_to(
        (place_of(query_block)[:, None] + row)[:, None, :], (tiles, head_count, BLK)
    ).reshape(tiles, head_count * BLK, 1)

    q = split_heads(queries, head_count)

    def both_cores(keys, distance, first=None, last=None):
        return [
            (keys, key_place[distance, 0, :, first:last]),
            (shift(keys, "k", 1), key_place[distance, 1, :, first:last]),
        ]

    half = near.shape[0] // 2
    down, up = shift(near, "y", 1), shift(near, "y", -1)
    state = attention(q, query_place, [both_cores(near, 0)], None, None, scale)
    down, up, gate_others[1], *state = tie(down, up, gate_others[1], *state)
    across = shift(down[:half], "y", 1), shift(up[half:], "y", -1)
    state = attention(q, query_place, [both_cores(up, 1), both_cores(down, 3)], state, None, scale)
    *across, state, w_o_own, gate_others[2] = tie(*across, state, w_o_own, gate_others[2])
    w_o_other = shift(w_o_own, "k", 1)
    groups = [both_cores(across[0], 2, None, half) + both_cores(across[1], 2, half, None)]
    heads = attention(q, query_place, groups, state, w_uv, scale)

    heads = heads.reshape(8, 2, token_count, heads.shape[1])
    mine = lax.dynamic_index_in_dim(heads, k, 1, keepdims=False)
    theirs = shift(lax.dynamic_index_in_dim(heads, 1 - k, 1, keepdims=False), "k", 1)
    both = jnp.stack([mine, theirs])
    both_other = shift(both, "xl", 1)
    both_other, lift_others[0] = tie(both_other, lift_others[0])
    first = jnp.where(xl == 0, both, both_other)
    second = jnp.where(xl == 0, both_other, both)
    rows = jnp.concatenate([first, second], axis=1).reshape(2, 16 * token_count, -1)
    w_o_own, w_down = tie(w_o_own, w_down)
    terms = project(rows[0], rows[1], w_o_own, w_o_other, token_count)
    down_width = model_width // NZ
    down_pieces = {}
    for step in range(NZ):
        piece = lax.dynamic_slice_in_dim(w_down[0], lax.rem(z - step + NZ, NZ) * down_width, down_width, 1)
        down_pieces[step] = shift(piece, "z", -step) if step else piece
    terms = with_some(terms, down_pieces, (1, 2, 6, 7))
    terms = lax.all_to_all(terms, ("xl", "xh", "y"), split_axis=0, concat_axis=0, tiled=True)
    terms = with_some(terms, down_pieces, (3, 5))
    projected = jnp.sum(terms.reshape((2, 8) + terms.shape[1:]).astype(jnp.float32), axis=1)
    projected = projected.reshape(2, NZ // 2, token_count, 2, column_count)
    projected = projected.transpose(2, 1, 3, 0, 4).reshape(token_count, model_width)

    attended = (residual.astype(jnp.float32) + projected).astype(jnp.bfloat16)
    level = attended.astype(jnp.float32)
    normed = (
        level
        * lax.rsqrt(jnp.mean(level * level, axis=1, keepdims=True) + 1e-06)
        * norm_gain.astype(jnp.float32)
    ).astype(jnp.bfloat16)

    share = 2.5 * route_scores / jnp.sum(route_scores, axis=1, keepdims=True)
    chosen = jnp.arange(owner_count, dtype=jnp.int32) * (EXPERTS // owner_count)
    match = routes[:, :, None] == chosen[None, None, :]
    hits = jnp.sum(match.astype(jnp.int32), axis=1)
    weight_to = jnp.sum(jnp.where(match, share[:, :, None], 0.0), axis=1)
    ranking = jnp.cumsum(hits, axis=0) - 1
    slot_ids = jnp.arange(CAP, dtype=jnp.int32)
    select = ((hits[:, :, None] == 1) & (ranking[:, :, None] == slot_ids[None, None, :])).astype(jnp.bfloat16)
    outgoing = jnp.einsum("toc,td->ocd", select, normed, preferred_element_type=jnp.float32).astype(jnp.bfloat16)
    arrived = lax.all_to_all(
        outgoing.reshape(owner_count * CAP, model_width), EXP, split_axis=0, concat_axis=0, tiled=True
    )
    arrived = with_some(arrived, down_pieces, (4,))
    arrived, lift_rest = tie(arrived, lift_own[early:])
    lift_others.append(shift(lift_rest, "xl", 1))
    x = lax.all_gather(arrived, "z", axis=0, tiled=True)
    down_own = pack([down_pieces[s] for s in range(NZ)])
    lift_others[1], down_own = tie(lift_others[1], down_own)
    down_other = shift(down_own, "xl", 1)
    hidden = hidden_units([x], gate_own, lift_own, gate_others, lift_others)
    down = up = hidden
    before, after = [], []
    for _ in range(1, NZ // 2):
        down, up = shift(down, "z", 1), shift(up, "z", -1)
        before.insert(0, down)
        after.append(up)
    half = hidden.shape[0] // 2
    pieces = [hidden] + after + [shift(down[:half], "z", 1), shift(up[half:], "z", -1)] + before
    lowered = lower(pieces, down_own, down_other)
    returned = lax.all_to_all(lowered, ("z",) + EXP, split_axis=0, concat_axis=0, tiled=True)
    returned = returned.reshape(NZ, owner_count, CAP, down_width)
    picked = jnp.einsum("toc,zocd->otzd", select, returned, preferred_element_type=jnp.float32)
    picked = picked.reshape(owner_count, token_count, model_width)
    expert_part = jnp.sum(picked * jnp.transpose(weight_to)[:, :, None], axis=0).astype(jnp.bfloat16)
    return (attended, expert_part)


def solution(mesh):
    fine = Mesh(mesh.devices.reshape(NZ, 2, 2, 4, 2), CTX + EXP)
    token = P(CTX + EXP, None)
    return jax.shard_map(
        per_device,
        mesh=fine,
        in_specs=(
            P(CTX, EXP),
            P(CTX, None),
            P(),
            P(EXP, None, None),
            P(EXP, CTX),
            token,
            P(),
            token,
            token,
            P(EXP, None, CTX),
            P(EXP, None, CTX),
            P(EXP, CTX, None),
        ),
        out_specs=(token, token),
        check_vma=False,
    )
```

```python
import functools
import math

import jax
import jax.numpy as jnp
from jax import lax
from jax.experimental import pallas as pl
from jax.experimental.pallas import tpu as pltpu
from jax.sharding import Mesh, PartitionSpec as P

EXPERTS = 256
BLK = 128
CAP = 2
LATENT = 512
PAIR = BLK // 8
WEIGHT_PART = 1024
NZ = 8
CTX = ("z", "xl")
EXP = ("xh", "y", "k")
VMEM_LIMIT = 20 * 2**20


def shift(value, axis, step):
    size = lax.axis_size(axis)
    return lax.ppermute(value, axis, [(i, (i + step) % size) for i in range(size)])


def tie(*values):
    return lax.optimization_barrier(values)


def with_some(value, pieces, steps):
    value, *ready = tie(value, *(pieces[s] for s in steps))
    pieces.update(zip(steps, ready))
    return value


def block_of(shape):
    return pl.BlockSpec(shape, lambda *_: (0,) * len(shape))


def split_kernel(in_ref, out_ref):
    heads = out_ref.shape[1] // in_ref.shape[0]
    tokens, width = in_ref.shape[0], in_ref.shape[1] // heads
    blank = jnp.zeros((tokens, 128 - (width - LATENT)), jnp.bfloat16)
    for head in range(heads):
        value = in_ref[:, head * width : (head + 1) * width]
        tail = value[:, LATENT:]
        rows = slice(head * tokens, (head + 1) * tokens)
        out_ref[0, rows, :LATENT] = value[:, :LATENT]
        out_ref[0, rows, LATENT : LATENT + 128] = jnp.concatenate([tail, blank], axis=1)
        out_ref[0, rows, LATENT + 128 :] = jnp.concatenate([blank, tail], axis=1)


def split_heads(queries, heads):
    rows, columns = queries.shape
    width = LATENT + 256
    return pl.pallas_call(
        split_kernel,
        grid=(rows // BLK,),
        out_shape=jax.ShapeDtypeStruct((rows // BLK, BLK * heads, width), jnp.bfloat16),
        in_specs=[pl.BlockSpec((BLK, columns), lambda i: (i, 0))],
        out_specs=pl.BlockSpec((1, BLK * heads, width), lambda i: (i, 0, 0)),
        compiler_params=pltpu.CompilerParams(vmem_limit_bytes=16 * 2**20),
        name="split",
    )(queries)


def paired(keys):
    half = keys.shape[0] // 2
    return jnp.concatenate(
        [keys[:half, :LATENT], keys[half:, :LATENT], keys[:half, LATENT:], keys[half:, LATENT:]], axis=1
    )


def attention_kernel(scale, groups, first, last, *refs):
    refs = list(refs)
    q_ref = refs.pop(0)
    query_place_ref = refs.pop(0)
    pieces = [[(refs.pop(0), refs.pop(0)) for _ in range(count)] for count in groups]
    factor = scale * math.log2(math.e)
    q = q_ref[0]
    q_first = q[:, : LATENT + 128]
    q_second = jnp.concatenate([q[:, :LATENT], q[:, LATENT + 128 :]], axis=1)
    rows = q.shape[0]
    query_place = query_place_ref[0]
    if first:
        highest = jnp.full((rows, 1), -1e29, jnp.float32)
        total = jnp.zeros((rows, 1), jnp.float32)
        mixed = jnp.zeros((rows, LATENT), jnp.float32)
    else:
        highest_ref, total_ref, mixed_ref = refs.pop(0), refs.pop(0), refs.pop(0)
        highest, total, mixed = highest_ref[0], total_ref[0], mixed_ref[0]
    for group in pieces:
        scores = []
        newest = highest
        for key_ref, place_ref in group:
            first_keys = jnp.concatenate([key_ref[:, :LATENT], key_ref[:, 2 * LATENT :]], axis=1)
            second_keys = key_ref[:, LATENT:]
            for keys, queries, offset in ((first_keys, q_first, 0), (second_keys, q_second, PAIR)):
                score = lax.dot_general(
                    queries, keys, (((1,), (1,)), ((), ())), preferred_element_type=jnp.float32
                )
                score = jnp.where(place_ref[...] + offset <= query_place, score * factor, -1e30)
                newest = jnp.maximum(newest, jnp.max(score, axis=1, keepdims=True))
                scores.append((score, key_ref, 0 if offset == 0 else LATENT))
        shrink = jnp.exp2(highest - newest)
        total = total * shrink
        mixed = mixed * shrink
        for score, key_ref, start in scores:
            weights = jnp.exp2(score - newest)
            total = total + jnp.sum(weights, axis=1, keepdims=True)
            mixed = mixed + jnp.dot(
                weights.astype(jnp.bfloat16),
                key_ref[:, start : start + LATENT],
                preferred_element_type=jnp.float32,
            )
        highest = newest
    if not last:
        highest_ref, total_ref, mixed_ref = refs
        highest_ref[0], total_ref[0], mixed_ref[0] = highest, total, mixed
        return
    w_uv_ref, out_ref = refs
    heads, _, value_width = w_uv_ref.shape
    mixed = (mixed / total).astype(jnp.bfloat16)
    tokens = rows // heads
    for head in range(heads):
        out_ref[:, head * value_width : (head + 1) * value_width] = jnp.dot(
            mixed[head * tokens : (head + 1) * tokens], w_uv_ref[head], preferred_element_type=jnp.float32
        ).astype(jnp.bfloat16)


def attention(q, query_place, groups, state, w_uv, scale):
    tiles, rows, key_width = q.shape
    whole = pl.BlockSpec(memory_space=pltpu.VMEM)
    tile = lambda *shape: pl.BlockSpec((1,) + shape, lambda i: (i,) + (0,) * len(shape))
    narrow, wide = tile(rows, 1), tile(rows, LATENT)
    flat = [v for group in groups for pair in group for v in pair]
    operands = [q, query_place] + flat
    specs = [tile(rows, key_width), narrow] + [whole] * len(flat)
    if state:
        operands += state
        specs += [narrow, narrow, wide]
    if w_uv is None:
        out_shape = [
            jax.ShapeDtypeStruct((tiles, rows, 1), jnp.float32),
            jax.ShapeDtypeStruct((tiles, rows, 1), jnp.float32),
            jax.ShapeDtypeStruct((tiles, rows, LATENT), jnp.float32),
        ]
        out_specs = [narrow, narrow, wide]
    else:
        heads, _, value_width = w_uv.shape
        operands.append(w_uv)
        specs.append(whole)
        out_shape = jax.ShapeDtypeStruct((tiles * rows // heads, heads * value_width), jnp.bfloat16)
        out_specs = pl.BlockSpec((rows // heads, heads * value_width), lambda i: (i, 0))
    keys = 2 * sum(pair[0].shape[0] for group in groups for pair in group)
    return pl.pallas_call(
        functools.partial(
            attention_kernel, scale, tuple(len(g) for g in groups), not state, w_uv is not None
        ),
        grid=(tiles,),
        out_shape=out_shape,
        in_specs=specs,
        out_specs=out_specs,
        compiler_params=pltpu.CompilerParams(vmem_limit_bytes=VMEM_LIMIT),
        name="attention",
    )(*operands)


def project_kernel(a_ref, b_ref, wa_ref, wb_ref, out_ref, held_a, held_b, sems):
    steps = out_ref.shape[1]
    copies = []
    for i in range(steps):
        pair = pl.ds(2 * i, 2)
        copies.append(
            (
                pltpu.make_async_copy(wa_ref.at[pair], held_a.at[pair], sems.at[0, i]),
                pltpu.make_async_copy(wb_ref.at[pair], held_b.at[pair], sems.at[1, i]),
            )
        )
        for copy in copies[-1]:
            copy.start()
    against = (((1,), (1,)), ((), ()))
    depth = a_ref.shape[1]
    for i in range(steps):
        term = 0.0
        for copy, held, ref in zip(copies[i], (held_a, held_b), (a_ref, b_ref)):
            copy.wait()
            term = term + lax.dot_general(
                ref[...], held[2 * i : 2 * i + 2].reshape(-1, depth), against, preferred_element_type=jnp.float32
            )
        groups, _, rows, columns = out_ref.shape
        out_ref[:, i] = term.astype(jnp.bfloat16).reshape(groups, rows, columns)


def project(a, b, wa, wb, group):
    rows, depth = a.shape
    count, columns, _ = wa.shape
    out = (rows // group, count // 2, group, 2 * columns)
    anywhere = pl.BlockSpec(memory_space=pl.ANY)
    return pl.pallas_call(
        project_kernel,
        grid=(1,),
        out_shape=jax.ShapeDtypeStruct(out, jnp.bfloat16),
        in_specs=[block_of(a.shape), block_of(b.shape), anywhere, anywhere],
        out_specs=block_of(out),
        scratch_shapes=[pltpu.VMEM(wa.shape, jnp.bfloat16)] * 2
        + [pltpu.SemaphoreType.DMA((2, count // 2))],
        compiler_params=pltpu.CompilerParams(vmem_limit_bytes=60 * 2**20),
        name="project",
    )(a, b, wa, wb)


def hidden_kernel(counts, *refs):
    *refs, out_ref, held, w_held, x_sems, w_sems = refs
    x_refs, refs = refs[: -sum(counts)], refs[-sum(counts) :]
    rows = x_refs[0].shape[0]
    x_copies = [
        pltpu.make_async_copy(ref, held.at[pl.ds(i * rows, rows)], x_sems.at[i]) for i, ref in enumerate(x_refs)
    ]
    for copy in x_copies:
        copy.start()
    steps = w_held.shape[1] // WEIGHT_PART
    copies = []
    for which, count in enumerate(counts):
        pieces, refs = refs[:count], refs[count:]
        at = 0
        for ref in pieces:
            for start in range(0, ref.shape[0], WEIGHT_PART):
                copies.append(
                    (
                        at,
                        pltpu.make_async_copy(
                            ref.at[pl.ds(start, WEIGHT_PART)],
                            w_held.at[which, pl.ds(at * WEIGHT_PART, WEIGHT_PART)],
                            w_sems.at[which, at],
                        ),
                    )
                )
                at += 1
    copies.sort(key=lambda pair: pair[0])
    for _, copy in copies:
        copy.start()
    for copy in x_copies:
        copy.wait()
    gate = lifted = 0.0
    for step in range(steps):
        for at, copy in copies:
            if at == step:
                copy.wait()
        part = slice(step * WEIGHT_PART, (step + 1) * WEIGHT_PART)
        x = held[:, part]
        gate = gate + jnp.dot(
            x, jnp.concatenate([w_held[0, part], w_held[1, part]], axis=1), preferred_element_type=jnp.float32
        )
        lifted = lifted + jnp.dot(
            x, jnp.concatenate([w_held[2, part], w_held[3, part]], axis=1), preferred_element_type=jnp.float32
        )
    out_ref[...] = (gate / (1.0 + jnp.exp(-gate)) * lifted).astype(jnp.bfloat16)


def hidden_units(xs, gate_own, lift_own, gate_others, lift_others):
    rows, depth = sum(x.shape[0] for x in xs), xs[0].shape[1]
    units = gate_own.shape[1]
    pieces = [[gate_own], gate_others, [lift_own], lift_others]
    flat = [v for group in pieces for v in group]
    return pl.pallas_call(
        functools.partial(hidden_kernel, tuple(len(group) for group in pieces)),
        grid=(1,),
        out_shape=jax.ShapeDtypeStruct((rows, 2 * units), jnp.bfloat16),
        in_specs=[pl.BlockSpec(memory_space=pl.ANY)] * (len(xs) + len(flat)),
        out_specs=block_of((rows, 2 * units)),
        scratch_shapes=[
            pltpu.VMEM((rows, depth), jnp.bfloat16),
            pltpu.VMEM((4, depth, units), jnp.bfloat16),
            pltpu.SemaphoreType.DMA((len(xs),)),
            pltpu.SemaphoreType.DMA((4, depth // WEIGHT_PART)),
        ],
        compiler_params=pltpu.CompilerParams(vmem_limit_bytes=60 * 2**20),
        name="hidden",
    )(*xs, *flat)


def pack_kernel(*refs):
    *in_refs, out_ref = refs
    for i, ref in enumerate(in_refs):
        out_ref[i] = ref[...]


def pack(pieces):
    whole = pl.BlockSpec(memory_space=pltpu.VMEM)
    return pl.pallas_call(
        pack_kernel,
        out_shape=jax.ShapeDtypeStruct((len(pieces),) + pieces[0].shape, pieces[0].dtype),
        in_specs=[whole] * len(pieces),
        out_specs=whole,
        compiler_params=pltpu.CompilerParams(vmem_limit_bytes=16 * 2**20),
        name="pack",
    )(*pieces)


def lower_kernel(*refs):
    *hidden_refs, own_ref, other_ref, out_ref = refs
    units = own_ref.shape[1]
    total = jnp.zeros(out_ref.shape, jnp.float32)
    for step in range(NZ):
        at = step
        piece = hidden_refs[step][...] if step < NZ // 2 else hidden_refs[step + 1][...]
        if step == NZ // 2:
            piece = jnp.concatenate([hidden_refs[step][...], piece], axis=0)
        total = total + jnp.dot(piece[:, :units], own_ref[at], preferred_element_type=jnp.float32)
        total = total + jnp.dot(piece[:, units:], other_ref[at], preferred_element_type=jnp.float32)
    out_ref[...] = total.astype(jnp.bfloat16)


def lower(pieces, own, other):
    rows = pieces[0].shape[0]
    columns = own.shape[2]
    whole = pl.BlockSpec(memory_space=pltpu.VMEM)
    return pl.pallas_call(
        lower_kernel,
        out_shape=jax.ShapeDtypeStruct((rows, columns), jnp.bfloat16),
        in_specs=[whole] * (len(pieces) + 2),
        out_specs=whole,
        compiler_params=pltpu.CompilerParams(vmem_limit_bytes=16 * 2**20),
        name="lower",
    )(*pieces, own, other)


def per_device(
    queries,
    latent,
    block_order,
    w_uv,
    w_o,
    residual,
    norm_gain,
    routes,
    route_scores,
    w_gate,
    w_up,
    w_down,
):
    z = lax.axis_index("z")
    xl = lax.axis_index("xl")
    y = lax.axis_index("y")
    k = lax.axis_index("k")
    owner_count = 16
    seq_block = queries.shape[0]
    head_count, latent_width, value_width = w_uv.shape
    key_width = latent.shape[1]
    token_count, model_width = residual.shape
    scale = (value_width + key_width - latent_width) ** (-0.5)
    tiles = seq_block // BLK
    column_count = w_o.shape[1]

    part = BLK // 4
    own = lax.dynamic_slice_in_dim(latent, k * BLK + y * part, part, 0)
    own = paired(own)
    other = shift(own, "xl", 1)
    gate_own, lift_own = w_gate[0], w_up[0]
    early = 3 * WEIGHT_PART
    pair = jnp.concatenate([own, other], axis=0)
    pair, gate_sent, lift_sent, w_o = tie(pair, gate_own, lift_own, w_o)
    cuts = [0, 4 * WEIGHT_PART, gate_sent.shape[0]]
    gate_others = [shift(gate_sent[i:j], "xl", 1) for i, j in zip(cuts, cuts[1:])]
    w_o_own = lax.all_gather(w_o.T, "z", axis=0)
    down, down2, up, up2 = (shift(pair, "z", s) for s in (1, 2, -1, -2))
    down3, up3 = shift(down2, "z", 1), shift(up2, "z", -1)
    far = jnp.concatenate([shift(down2[:PAIR], "z", 2), shift(up2[PAIR:], "z", -2)], axis=0)
    near = pack([down3, down2, down, pair, up, up2, up3, far]).reshape(-1, pair.shape[1])
    near, lift_sent, gate_others[0] = tie(near, lift_sent, gate_others[0])
    lift_others = [shift(lift_sent[:early], "xl", 1)]

    turn = jnp.arange(2, dtype=jnp.int32)
    where = (z + jnp.arange(1 - NZ // 2, NZ // 2 + 1, dtype=jnp.int32)) % NZ
    key_block = 2 * (2 * where[:, None] + (xl ^ turn)) + (k ^ turn[:, None, None])
    table = jnp.arange(block_order.shape[0], dtype=jnp.int32)

    def place_of(block):
        pick = block[..., None] == table
        return jnp.sum(jnp.where(pick, block_order, 0), axis=-1) * BLK

    row = jnp.arange(BLK, dtype=jnp.int32)
    key_place = place_of(key_block) + ((y + jnp.arange(4, dtype=jnp.int32)) % 4 * part)[
        :, None, None, None
    ]
    key_place = (key_place[..., None] + row[:PAIR]).reshape(4, 2, 1, -1)
    query_block = 2 * (2 * z + xl) + jnp.arange(tiles, dtype=jnp.int32)
    query_place = jnp.broadcast_to(
        (place_of(query_block)[:, None] + row)[:, None, :], (tiles, head_count, BLK)
    ).reshape(tiles, head_count * BLK, 1)

    q = split_heads(queries, head_count)

    def both_cores(keys, distance, first=None, last=None):
        return [
            (keys, key_place[distance, 0, :, first:last]),
            (shift(keys, "k", 1), key_place[distance, 1, :, first:last]),
        ]

    half = near.shape[0] // 2
    down, up = shift(near, "y", 1), shift(near, "y", -1)
    state = attention(q, query_place, [both_cores(near, 0)], None, None, scale)
    down, up, gate_others[1], *state = tie(down, up, gate_others[1], *state)
    across = shift(down[:half], "y", 1), shift(up[half:], "y", -1)
    state = attention(q, query_place, [both_cores(up, 1), both_cores(down, 3)], state, None, scale)
    *across, state, w_o_own = tie(*across, state, w_o_own)
    w_o_other = shift(w_o_own, "k", 1)
    groups = [both_cores(across[0], 2, None, half) + both_cores(across[1], 2, half, None)]
    heads = attention(q, query_place, groups, state, w_uv, scale)

    heads = heads.reshape(8, 2, token_count, heads.shape[1])
    mine = lax.dynamic_index_in_dim(heads, k, 1, keepdims=False)
    theirs = shift(lax.dynamic_index_in_dim(heads, 1 - k, 1, keepdims=False), "k", 1)
    both = jnp.stack([mine, theirs])
    both_other = shift(both, "xl", 1)
    both_other, lift_others[0] = tie(both_other, lift_others[0])
    first = jnp.where(xl == 0, both, both_other)
    second = jnp.where(xl == 0, both_other, both)
    rows = jnp.concatenate([first, second], axis=1).reshape(2, 16 * token_count, -1)
    w_o_own, w_down = tie(w_o_own, w_down)
    terms = project(rows[0], rows[1], w_o_own, w_o_other, token_count)
    down_width = model_width // NZ
    down_pieces = {}
    for step in range(NZ):
        piece = lax.dynamic_slice_in_dim(w_down[0], lax.rem(z - step + NZ, NZ) * down_width, down_width, 1)
        down_pieces[step] = shift(piece, "z", -step) if step else piece
    terms = with_some(terms, down_pieces, (1, 6, 7))
    terms = lax.all_to_all(terms, ("xl", "xh", "y"), split_axis=0, concat_axis=0, tiled=True)
    terms = with_some(terms, down_pieces, (3, 5))
    projected = jnp.sum(terms.reshape((2, 8) + terms.shape[1:]).astype(jnp.float32), axis=1)
    projected = projected.reshape(2, NZ // 2, token_count, 2, column_count)
    projected = projected.transpose(2, 1, 3, 0, 4).reshape(token_count, model_width)

    attended = (residual.astype(jnp.float32) + projected).astype(jnp.bfloat16)
    level = attended.astype(jnp.float32)
    normed = (
        level
        * lax.rsqrt(jnp.mean(level * level, axis=1, keepdims=True) + 1e-06)
        * norm_gain.astype(jnp.float32)
    ).astype(jnp.bfloat16)

    share = 2.5 * route_scores / jnp.sum(route_scores, axis=1, keepdims=True)
    chosen = jnp.arange(owner_count, dtype=jnp.int32) * (EXPERTS // owner_count)
    match = routes[:, :, None] == chosen[None, None, :]
    hits = jnp.sum(match.astype(jnp.int32), axis=1)
    weight_to = jnp.sum(jnp.where(match, share[:, :, None], 0.0), axis=1)
    ranking = jnp.cumsum(hits, axis=0) - 1
    slot_ids = jnp.arange(CAP, dtype=jnp.int32)
    select = ((hits[:, :, None] == 1) & (ranking[:, :, None] == slot_ids[None, None, :])).astype(jnp.bfloat16)
    outgoing = jnp.einsum("toc,td->ocd", select, normed, preferred_element_type=jnp.float32).astype(jnp.bfloat16)
    arrived = lax.all_to_all(
        outgoing.reshape(owner_count * CAP, model_width), EXP, split_axis=0, concat_axis=0, tiled=True
    )
    arrived = with_some(arrived, down_pieces, (2, 4))
    arrived, lift_rest = tie(arrived, lift_own[early:])
    lift_others.append(shift(lift_rest, "xl", 1))
    x = lax.all_gather(arrived, "z", axis=0, tiled=True)
    down_own = pack([down_pieces[s] for s in range(NZ)])
    lift_others[1], down_own = tie(lift_others[1], down_own)
    down_other = shift(down_own, "xl", 1)
    hidden = hidden_units([x], gate_own, lift_own, gate_others, lift_others)
    down = up = hidden
    before, after = [], []
    for _ in range(1, NZ // 2):
        down, up = shift(down, "z", 1), shift(up, "z", -1)
        before.insert(0, down)
        after.append(up)
    half = hidden.shape[0] // 2
    pieces = [hidden] + after + [shift(down[:half], "z", 1), shift(up[half:], "z", -1)] + before
    lowered = lower(pieces, down_own, down_other)
    returned = lax.all_to_all(lowered, ("z",) + EXP, split_axis=0, concat_axis=0, tiled=True)
    returned = returned.reshape(NZ, owner_count, CAP, down_width)
    picked = jnp.einsum("toc,zocd->otzd", select, returned, preferred_element_type=jnp.float32)
    picked = picked.reshape(owner_count, token_count, model_width)
    expert_part = jnp.sum(picked * jnp.transpose(weight_to)[:, :, None], axis=0).astype(jnp.bfloat16)
    return (attended, expert_part)


def solution(mesh):
    fine = Mesh(mesh.devices.reshape(NZ, 2, 2, 4, 2), CTX + EXP)
    token = P(CTX + EXP, None)
    return jax.shard_map(
        per_device,
        mesh=fine,
        in_specs=(
            P(CTX, EXP),
            P(CTX, None),
            P(),
            P(EXP, None, None),
            P(EXP, CTX),
            token,
            P(),
            token,
            token,
            P(EXP, None, CTX),
            P(EXP, None, CTX),
            P(EXP, CTX, None),
        ),
        out_specs=(token, token),
        check_vma=False,
    )
```

```python
import functools
import math

import jax
import jax.numpy as jnp
from jax import lax
from jax.experimental import pallas as pl
from jax.experimental.pallas import tpu as pltpu
from jax.sharding import Mesh, PartitionSpec as P

EXPERTS = 256
BLK = 128
CAP = 2
LATENT = 512
PAIR = BLK // 8
WEIGHT_PART = 1024
NZ = 8
CTX = ("z", "xl")
EXP = ("xh", "y", "k")
VMEM_LIMIT = 20 * 2**20


def shift(value, axis, step):
    size = lax.axis_size(axis)
    return lax.ppermute(value, axis, [(i, (i + step) % size) for i in range(size)])


def tie(*values):
    return lax.optimization_barrier(values)


def with_some(value, pieces, steps):
    value, *ready = tie(value, *(pieces[s] for s in steps))
    pieces.update(zip(steps, ready))
    return value


def block_of(shape):
    return pl.BlockSpec(shape, lambda *_: (0,) * len(shape))


def split_kernel(in_ref, out_ref):
    heads = out_ref.shape[1] // in_ref.shape[0]
    tokens, width = in_ref.shape[0], in_ref.shape[1] // heads
    blank = jnp.zeros((tokens, 128 - (width - LATENT)), jnp.bfloat16)
    for head in range(heads):
        value = in_ref[:, head * width : (head + 1) * width]
        tail = value[:, LATENT:]
        rows = slice(head * tokens, (head + 1) * tokens)
        out_ref[0, rows, :LATENT] = value[:, :LATENT]
        out_ref[0, rows, LATENT : LATENT + 128] = jnp.concatenate([tail, blank], axis=1)
        out_ref[0, rows, LATENT + 128 :] = jnp.concatenate([blank, tail], axis=1)


def split_heads(queries, heads):
    rows, columns = queries.shape
    width = LATENT + 256
    return pl.pallas_call(
        split_kernel,
        grid=(rows // BLK,),
        out_shape=jax.ShapeDtypeStruct((rows // BLK, BLK * heads, width), jnp.bfloat16),
        in_specs=[pl.BlockSpec((BLK, columns), lambda i: (i, 0))],
        out_specs=pl.BlockSpec((1, BLK * heads, width), lambda i: (i, 0, 0)),
        compiler_params=pltpu.CompilerParams(vmem_limit_bytes=16 * 2**20),
        name="split",
    )(queries)


def paired(keys):
    half = keys.shape[0] // 2
    return jnp.concatenate(
        [keys[:half, :LATENT], keys[half:, :LATENT], keys[:half, LATENT:], keys[half:, LATENT:]], axis=1
    )


def attention_kernel(scale, groups, first, last, *refs):
    refs = list(refs)
    q_ref = refs.pop(0)
    query_place_ref = refs.pop(0)
    pieces = [[(refs.pop(0), refs.pop(0)) for _ in range(count)] for count in groups]
    factor = scale * math.log2(math.e)
    q = q_ref[0]
    q_first = q[:, : LATENT + 128]
    q_second = jnp.concatenate([q[:, :LATENT], q[:, LATENT + 128 :]], axis=1)
    rows = q.shape[0]
    query_place = query_place_ref[0]
    if first:
        highest = jnp.full((rows, 1), -1e29, jnp.float32)
        total = jnp.zeros((rows, 1), jnp.float32)
        mixed = jnp.zeros((rows, LATENT), jnp.float32)
    else:
        highest_ref, total_ref, mixed_ref = refs.pop(0), refs.pop(0), refs.pop(0)
        highest, total, mixed = highest_ref[0], total_ref[0], mixed_ref[0]
    for group in pieces:
        scores = []
        newest = highest
        for key_ref, place_ref in group:
            first_keys = jnp.concatenate([key_ref[:, :LATENT], key_ref[:, 2 * LATENT :]], axis=1)
            second_keys = key_ref[:, LATENT:]
            for keys, queries, offset in ((first_keys, q_first, 0), (second_keys, q_second, PAIR)):
                score = lax.dot_general(
                    queries, keys, (((1,), (1,)), ((), ())), preferred_element_type=jnp.float32
                )
                score = jnp.where(place_ref[...] + offset <= query_place, score * factor, -1e30)
                newest = jnp.maximum(newest, jnp.max(score, axis=1, keepdims=True))
                scores.append((score, key_ref, 0 if offset == 0 else LATENT))
        shrink = jnp.exp2(highest - newest)
        total = total * shrink
        mixed = mixed * shrink
        for score, key_ref, start in scores:
            weights = jnp.exp2(score - newest)
            total = total + jnp.sum(weights, axis=1, keepdims=True)
            mixed = mixed + jnp.dot(
                weights.astype(jnp.bfloat16),
                key_ref[:, start : start + LATENT],
                preferred_element_type=jnp.float32,
            )
        highest = newest
    if not last:
        highest_ref, total_ref, mixed_ref = refs
        highest_ref[0], total_ref[0], mixed_ref[0] = highest, total, mixed
        return
    w_uv_ref, out_ref = refs
    heads, _, value_width = w_uv_ref.shape
    mixed = (mixed / total).astype(jnp.bfloat16)
    tokens = rows // heads
    for head in range(heads):
        out_ref[:, head * value_width : (head + 1) * value_width] = jnp.dot(
            mixed[head * tokens : (head + 1) * tokens], w_uv_ref[head], preferred_element_type=jnp.float32
        ).astype(jnp.bfloat16)


def attention(q, query_place, groups, state, w_uv, scale):
    tiles, rows, key_width = q.shape
    whole = pl.BlockSpec(memory_space=pltpu.VMEM)
    tile = lambda *shape: pl.BlockSpec((1,) + shape, lambda i: (i,) + (0,) * len(shape))
    narrow, wide = tile(rows, 1), tile(rows, LATENT)
    flat = [v for group in groups for pair in group for v in pair]
    operands = [q, query_place] + flat
    specs = [tile(rows, key_width), narrow] + [whole] * len(flat)
    if state:
        operands += state
        specs += [narrow, narrow, wide]
    if w_uv is None:
        out_shape = [
            jax.ShapeDtypeStruct((tiles, rows, 1), jnp.float32),
            jax.ShapeDtypeStruct((tiles, rows, 1), jnp.float32),
            jax.ShapeDtypeStruct((tiles, rows, LATENT), jnp.float32),
        ]
        out_specs = [narrow, narrow, wide]
    else:
        heads, _, value_width = w_uv.shape
        operands.append(w_uv)
        specs.append(whole)
        out_shape = jax.ShapeDtypeStruct((tiles * rows // heads, heads * value_width), jnp.bfloat16)
        out_specs = pl.BlockSpec((rows // heads, heads * value_width), lambda i: (i, 0))
    keys = 2 * sum(pair[0].shape[0] for group in groups for pair in group)
    return pl.pallas_call(
        functools.partial(
            attention_kernel, scale, tuple(len(g) for g in groups), not state, w_uv is not None
        ),
        grid=(tiles,),
        out_shape=out_shape,
        in_specs=specs,
        out_specs=out_specs,
        compiler_params=pltpu.CompilerParams(vmem_limit_bytes=VMEM_LIMIT),
        name="attention",
    )(*operands)


def project_kernel(a_ref, b_ref, wa_ref, wb_ref, out_ref, held_a, held_b, sems):
    steps = out_ref.shape[1]
    copies = []
    for i in range(steps):
        pair = pl.ds(2 * i, 2)
        copies.append(
            (
                pltpu.make_async_copy(wa_ref.at[pair], held_a.at[pair], sems.at[0, i]),
                pltpu.make_async_copy(wb_ref.at[pair], held_b.at[pair], sems.at[1, i]),
            )
        )
        for copy in copies[-1]:
            copy.start()
    against = (((1,), (1,)), ((), ()))
    depth = a_ref.shape[1]
    for i in range(steps):
        term = 0.0
        for copy, held, ref in zip(copies[i], (held_a, held_b), (a_ref, b_ref)):
            copy.wait()
            term = term + lax.dot_general(
                ref[...], held[2 * i : 2 * i + 2].reshape(-1, depth), against, preferred_element_type=jnp.float32
            )
        groups, _, rows, columns = out_ref.shape
        out_ref[:, i] = term.astype(jnp.bfloat16).reshape(groups, rows, columns)


def project(a, b, wa, wb, group):
    rows, depth = a.shape
    count, columns, _ = wa.shape
    out = (rows // group, count // 2, group, 2 * columns)
    anywhere = pl.BlockSpec(memory_space=pl.ANY)
    return pl.pallas_call(
        project_kernel,
        grid=(1,),
        out_shape=jax.ShapeDtypeStruct(out, jnp.bfloat16),
        in_specs=[block_of(a.shape), block_of(b.shape), anywhere, anywhere],
        out_specs=block_of(out),
        scratch_shapes=[pltpu.VMEM(wa.shape, jnp.bfloat16)] * 2
        + [pltpu.SemaphoreType.DMA((2, count // 2))],
        compiler_params=pltpu.CompilerParams(vmem_limit_bytes=60 * 2**20),
        name="project",
    )(a, b, wa, wb)


def hidden_kernel(counts, *refs):
    *refs, out_ref, held, w_held, x_sems, w_sems = refs
    x_refs, refs = refs[: -sum(counts)], refs[-sum(counts) :]
    rows = x_refs[0].shape[0]
    x_copies = [
        pltpu.make_async_copy(ref, held.at[pl.ds(i * rows, rows)], x_sems.at[i]) for i, ref in enumerate(x_refs)
    ]
    for copy in x_copies:
        copy.start()
    steps = w_held.shape[1] // WEIGHT_PART
    copies = []
    for which, count in enumerate(counts):
        pieces, refs = refs[:count], refs[count:]
        at = 0
        for ref in pieces:
            for start in range(0, ref.shape[0], WEIGHT_PART):
                copies.append(
                    (
                        at,
                        pltpu.make_async_copy(
                            ref.at[pl.ds(start, WEIGHT_PART)],
                            w_held.at[which, pl.ds(at * WEIGHT_PART, WEIGHT_PART)],
                            w_sems.at[which, at],
                        ),
                    )
                )
                at += 1
    copies.sort(key=lambda pair: pair[0])
    for _, copy in copies:
        copy.start()
    for copy in x_copies:
        copy.wait()
    gate = lifted = 0.0
    for step in range(steps):
        for at, copy in copies:
            if at == step:
                copy.wait()
        part = slice(step * WEIGHT_PART, (step + 1) * WEIGHT_PART)
        x = held[:, part]
        gate = gate + jnp.dot(
            x, jnp.concatenate([w_held[0, part], w_held[1, part]], axis=1), preferred_element_type=jnp.float32
        )
        lifted = lifted + jnp.dot(
            x, jnp.concatenate([w_held[2, part], w_held[3, part]], axis=1), preferred_element_type=jnp.float32
        )
    out_ref[...] = (gate / (1.0 + jnp.exp(-gate)) * lifted).astype(jnp.bfloat16)


def hidden_units(xs, gate_own, lift_own, gate_others, lift_others):
    rows, depth = sum(x.shape[0] for x in xs), xs[0].shape[1]
    units = gate_own.shape[1]
    pieces = [[gate_own], gate_others, [lift_own], lift_others]
    flat = [v for group in pieces for v in group]
    return pl.pallas_call(
        functools.partial(hidden_kernel, tuple(len(group) for group in pieces)),
        grid=(1,),
        out_shape=jax.ShapeDtypeStruct((rows, 2 * units), jnp.bfloat16),
        in_specs=[pl.BlockSpec(memory_space=pl.ANY)] * (len(xs) + len(flat)),
        out_specs=block_of((rows, 2 * units)),
        scratch_shapes=[
            pltpu.VMEM((rows, depth), jnp.bfloat16),
            pltpu.VMEM((4, depth, units), jnp.bfloat16),
            pltpu.SemaphoreType.DMA((len(xs),)),
            pltpu.SemaphoreType.DMA((4, depth // WEIGHT_PART)),
        ],
        compiler_params=pltpu.CompilerParams(vmem_limit_bytes=60 * 2**20),
        name="hidden",
    )(*xs, *flat)


def pack_kernel(*refs):
    *in_refs, out_ref = refs
    for i, ref in enumerate(in_refs):
        out_ref[i] = ref[...]


def pack(pieces):
    whole = pl.BlockSpec(memory_space=pltpu.VMEM)
    return pl.pallas_call(
        pack_kernel,
        out_shape=jax.ShapeDtypeStruct((len(pieces),) + pieces[0].shape, pieces[0].dtype),
        in_specs=[whole] * len(pieces),
        out_specs=whole,
        compiler_params=pltpu.CompilerParams(vmem_limit_bytes=16 * 2**20),
        name="pack",
    )(*pieces)


def lower_kernel(*refs):
    *hidden_refs, own_ref, other_ref, out_ref = refs
    units = own_ref.shape[1]
    total = jnp.zeros(out_ref.shape, jnp.float32)
    for step in range(NZ):
        at = step
        piece = hidden_refs[step][...] if step < NZ // 2 else hidden_refs[step + 1][...]
        if step == NZ // 2:
            piece = jnp.concatenate([hidden_refs[step][...], piece], axis=0)
        total = total + jnp.dot(piece[:, :units], own_ref[at], preferred_element_type=jnp.float32)
        total = total + jnp.dot(piece[:, units:], other_ref[at], preferred_element_type=jnp.float32)
    out_ref[...] = total.astype(jnp.bfloat16)


def lower(pieces, own, other):
    rows = pieces[0].shape[0]
    columns = own.shape[2]
    whole = pl.BlockSpec(memory_space=pltpu.VMEM)
    return pl.pallas_call(
        lower_kernel,
        out_shape=jax.ShapeDtypeStruct((rows, columns), jnp.bfloat16),
        in_specs=[whole] * (len(pieces) + 2),
        out_specs=whole,
        compiler_params=pltpu.CompilerParams(vmem_limit_bytes=16 * 2**20),
        name="lower",
    )(*pieces, own, other)


def per_device(
    queries,
    latent,
    block_order,
    w_uv,
    w_o,
    residual,
    norm_gain,
    routes,
    route_scores,
    w_gate,
    w_up,
    w_down,
):
    z = lax.axis_index("z")
    xl = lax.axis_index("xl")
    y = lax.axis_index("y")
    k = lax.axis_index("k")
    owner_count = 16
    seq_block = queries.shape[0]
    head_count, latent_width, value_width = w_uv.shape
    key_width = latent.shape[1]
    token_count, model_width = residual.shape
    scale = (value_width + key_width - latent_width) ** (-0.5)
    tiles = seq_block // BLK
    column_count = w_o.shape[1]

    part = BLK // 4
    own = lax.dynamic_slice_in_dim(latent, k * BLK + y * part, part, 0)
    own = paired(own)
    other = shift(own, "xl", 1)
    gate_own, lift_own = w_gate[0], w_up[0]
    early = 3 * WEIGHT_PART
    pair = jnp.concatenate([own, other], axis=0)
    pair, gate_sent, lift_sent, w_o = tie(pair, gate_own, lift_own, w_o)
    cuts = [0, 4 * WEIGHT_PART, gate_sent.shape[0]]
    gate_others = [shift(gate_sent[i:j], "xl", 1) for i, j in zip(cuts, cuts[1:])]
    w_o_own = lax.all_gather(w_o.T, "z", axis=0)
    down, down2, up, up2 = (shift(pair, "z", s) for s in (1, 2, -1, -2))
    down3, up3 = shift(down2, "z", 1), shift(up2, "z", -1)
    far = jnp.concatenate([shift(down2[:PAIR], "z", 2), shift(up2[PAIR:], "z", -2)], axis=0)
    near = pack([down3, down2, down, pair, up, up2, up3, far]).reshape(-1, pair.shape[1])
    near, lift_sent, gate_others[0] = tie(near, lift_sent, gate_others[0])
    lift_others = [shift(lift_sent[:early], "xl", 1)]

    turn = jnp.arange(2, dtype=jnp.int32)
    where = (z + jnp.arange(1 - NZ // 2, NZ // 2 + 1, dtype=jnp.int32)) % NZ
    key_block = 2 * (2 * where[:, None] + (xl ^ turn)) + (k ^ turn[:, None, None])
    table = jnp.arange(block_order.shape[0], dtype=jnp.int32)

    def place_of(block):
        pick = block[..., None] == table
        return jnp.sum(jnp.where(pick, block_order, 0), axis=-1) * BLK

    row = jnp.arange(BLK, dtype=jnp.int32)
    key_place = place_of(key_block) + ((y + jnp.arange(4, dtype=jnp.int32)) % 4 * part)[
        :, None, None, None
    ]
    key_place = (key_place[..., None] + row[:PAIR]).reshape(4, 2, 1, -1)
    query_block = 2 * (2 * z + xl) + jnp.arange(tiles, dtype=jnp.int32)
    query_place = jnp.broadcast_to(
        (place_of(query_block)[:, None] + row)[:, None, :], (tiles, head_count, BLK)
    ).reshape(tiles, head_count * BLK, 1)

    q = split_heads(queries, head_count)

    def both_cores(keys, distance, first=None, last=None):
        return [
            (keys, key_place[distance, 0, :, first:last]),
            (shift(keys, "k", 1), key_place[distance, 1, :, first:last]),
        ]

    half = near.shape[0] // 2
    down, up = shift(near, "y", 1), shift(near, "y", -1)
    state = attention(q, query_place, [both_cores(near, 0)], None, None, scale)
    down, up, gate_others[1], *state = tie(down, up, gate_others[1], *state)
    across = shift(down[:half], "y", 1), shift(up[half:], "y", -1)
    state = attention(q, query_place, [both_cores(up, 1), both_cores(down, 3)], state, None, scale)
    *across, state, w_o_own = tie(*across, state, w_o_own)
    w_o_other = shift(w_o_own, "k", 1)
    groups = [both_cores(across[0], 2, None, half) + both_cores(across[1], 2, half, None)]
    heads = attention(q, query_place, groups, state, w_uv, scale)

    heads = heads.reshape(8, 2, token_count, heads.shape[1])
    mine = lax.dynamic_index_in_dim(heads, k, 1, keepdims=False)
    theirs = shift(lax.dynamic_index_in_dim(heads, 1 - k, 1, keepdims=False), "k", 1)
    both = jnp.stack([mine, theirs])
    both_other = shift(both, "xl", 1)
    both_other, lift_others[0] = tie(both_other, lift_others[0])
    first = jnp.where(xl == 0, both, both_other)
    second = jnp.where(xl == 0, both_other, both)
    rows = jnp.concatenate([first, second], axis=1).reshape(2, 16 * token_count, -1)
    w_o_own, w_down = tie(w_o_own, w_down)
    terms = project(rows[0], rows[1], w_o_own, w_o_other, token_count)
    down_width = model_width // NZ
    down_pieces = {}
    for step in range(NZ):
        piece = lax.dynamic_slice_in_dim(w_down[0], lax.rem(z - step + NZ, NZ) * down_width, down_width, 1)
        down_pieces[step] = shift(piece, "z", -step) if step else piece
    terms = with_some(terms, down_pieces, (1, 6, 7))
    terms = lax.all_to_all(terms, ("xl", "xh", "y"), split_axis=0, concat_axis=0, tiled=True)
    terms = with_some(terms, down_pieces, (3, 5))
    projected = jnp.sum(terms.reshape((2, 8) + terms.shape[1:]).astype(jnp.float32), axis=1)
    projected = projected.reshape(2, NZ // 2, token_count, 2, column_count)
    projected = projected.transpose(2, 1, 3, 0, 4).reshape(token_count, model_width)

    attended = (residual.astype(jnp.float32) + projected).astype(jnp.bfloat16)
    level = attended.astype(jnp.float32)
    normed = (
        level
        * lax.rsqrt(jnp.mean(level * level, axis=1, keepdims=True) + 1e-06)
        * norm_gain.astype(jnp.float32)
    ).astype(jnp.bfloat16)

    share = 2.5 * route_scores / jnp.sum(route_scores, axis=1, keepdims=True)
    chosen = jnp.arange(owner_count, dtype=jnp.int32) * (EXPERTS // owner_count)
    match = routes[:, :, None] == chosen[None, None, :]
    hits = jnp.sum(match.astype(jnp.int32), axis=1)
    weight_to = jnp.sum(jnp.where(match, share[:, :, None], 0.0), axis=1)
    ranking = jnp.cumsum(hits, axis=0) - 1
    slot_ids = jnp.arange(CAP, dtype=jnp.int32)
    select = ((hits[:, :, None] == 1) & (ranking[:, :, None] == slot_ids[None, None, :])).astype(jnp.bfloat16)
    outgoing = jnp.einsum("toc,td->ocd", select, normed, preferred_element_type=jnp.float32).astype(jnp.bfloat16)
    arrived = lax.all_to_all(
        outgoing.reshape(owner_count * CAP, model_width), EXP, split_axis=0, concat_axis=0, tiled=True
    )
    arrived = with_some(arrived, down_pieces, (2, 4))
    arrived, lift_rest = tie(arrived, lift_own[early:])
    lift_others.append(shift(lift_rest, "xl", 1))
    x = lax.all_gather(arrived, "z", axis=0, tiled=True)
    down_own = pack([down_pieces[s] for s in range(NZ)])
    lift_others[1], down_own = tie(lift_others[1], down_own)
    down_other = shift(down_own, "xl", 1)
    hidden = hidden_units([x], gate_own, lift_own, gate_others, lift_others)
    down, down2, up, up2 = (shift(hidden, "z", step) for step in (1, 2, -1, -2))
    down3, up3 = shift(down2, "z", 1), shift(up2, "z", -1)
    half = hidden.shape[0] // 2
    far = [shift(down2[:half], "z", 2), shift(up2[half:], "z", -2)]
    pieces = [hidden, up, up2, up3] + far + [down3, down2, down]
    lowered = lower(pieces, down_own, down_other)
    returned = lax.all_to_all(lowered, ("z",) + EXP, split_axis=0, concat_axis=0, tiled=True)
    returned = returned.reshape(NZ, owner_count, CAP, down_width)
    picked = jnp.einsum("toc,zocd->otzd", select, returned, preferred_element_type=jnp.float32)
    picked = picked.reshape(owner_count, token_count, model_width)
    expert_part = jnp.sum(picked * jnp.transpose(weight_to)[:, :, None], axis=0).astype(jnp.bfloat16)
    return (attended, expert_part)


def solution(mesh):
    fine = Mesh(mesh.devices.reshape(NZ, 2, 2, 4, 2), CTX + EXP)
    token = P(CTX + EXP, None)
    return jax.shard_map(
        per_device,
        mesh=fine,
        in_specs=(
            P(CTX, EXP),
            P(CTX, None),
            P(),
            P(EXP, None, None),
            P(EXP, CTX),
            token,
            P(),
            token,
            token,
            P(EXP, None, CTX),
            P(EXP, None, CTX),
            P(EXP, CTX, None),
        ),
        out_specs=(token, token),
        check_vma=False,
    )
```
